512 devices in a mesh: dp: 64 (over x, z, core), graph: 8 (over y).
Axes of the slice: x: 4, y: 8, z: 8, core: 2. Of those that a mesh axis runs over, the one named last changes fastest.
Arguments:
- texts: bfloat16 [2048, 128, 768], P(('dp', 'graph')), may hold values from -48 to 48
- qkv_weight: bfloat16 [768, 2304], P(None, 'dp'), may hold values from -0.21875 to 0.21875
- norm_gain: float32 [768], replicated, may hold values from 0.1 to 1.9
- routes: int32 [2048, 8], P(('dp', 'graph')), may hold values from 0 to 63, all different within a row; in each aligned block of 4 rows (0 to 3, 4 to 7, ...) at most 2 rows name the same one
- w_self: float32 [768, 1024], P(None, 'graph'), may hold values from -0.21875 to 0.21875
- w_neigh: float32 [768, 1024], P(None, 'graph'), may hold values from -0.21875 to 0.21875
- gnn_bias: float32 [1024], P('graph'), may hold values from -3 to 3
- neighbors: int32 [65536, 15], P('dp'), may hold values from 0 to 1023
- cotangent: float32 [65536, 1024], P('dp', 'graph'), may hold values from -6 to 6
Outputs:
- hidden_nodes: float32 [65536, 1024], P('dp', 'graph')
- node_grads: float32 [2048, 768], P(('dp', 'graph'))
The draws below stay inside these ranges and needn't reach their ends.
Inputs may be any that keep to these rules, and one draw needn't show every extreme that they name: `routes`: in each aligned block of 4 rows no partition is named more than 2 times, and a row never names a partition twice.
All inputs are finite; a program needn't handle non-finite values.
Results may differ from the reference program's by a relative error of at most 0.012.
The reference program's roundings to bfloat16 on the way count: a program that leaves them out, or rounds other values in their place, can miss the bound.
Values may be sent and summed in bfloat16 or wider, within the bound.
A program may use at most 64 MiB of HBM per device.

```python
import math
import jax
import jax.numpy as jnp
import numpy as np
from jax import lax

D = 768
HEADS = 12
HID = 1024
SEQ = 128
COPIES = 8
FAN = 15
TITLES_DEV = 4
CAP = 2
SLOTS = 128
PART_ROWS = 1024
TITLES = 2048
N_DP = 64
N_GRAPH = 8


def draw_texts(key, part):
    key = jax.random.fold_in(key, 11)
    base_key = jax.random.fold_in(key, 0)
    values = jax.random.normal(base_key, (TITLES, SEQ, D), jnp.float32)
    values = jnp.clip(values, -6.0, 6.0)
    return values.astype(jnp.bfloat16)


def plant(values, own_key, smallest, top_value):
    longest = values.shape.index(max(values.shape))
    spots = []
    for shift in (0, 1):
        where = [jax.random.randint(jax.random.fold_in(own_key, axis), (), 0, length) for axis, length in enumerate(values.shape)]
        where[longest] = (where[longest] + shift) % values.shape[longest]
        spots.append(tuple(where))
    return values.at[spots[0]].set(smallest).at[spots[1]].set(top_value)


def levels(key, dims, shards, smallest, top_value):
    gain = 1.0
    for axis_at, parts in shards:
        steps = jax.random.uniform(jax.random.fold_in(jax.random.fold_in(key, 6), axis_at), (parts,), jnp.float32, smallest / len(shards), top_value / len(shards))
        gain = gain * jnp.repeat(jnp.exp(steps), dims[axis_at] // parts).reshape((-1,) + (1,) * (len(dims) - 1 - axis_at))
    return gain


def assign_block(stream_key, own, number, rows, number_of, top, limit, lean):
    order = jax.random.permutation(stream_key, number_of)
    crowded, usual = load_shares(number_of, rows * top, limit, lean, True), load_shares(number_of, rows * top, limit, lean, False)
    places = jnp.arange(number_of)

    def named(tallies, offset_by):
        used = int((tallies > 0).sum())
        fixed = max(1, used // 4)
        shifted = fixed + (places - fixed + offset_by * (used - fixed)) % max(1, number_of - fixed)
        return jnp.zeros((number_of,), jnp.int32).at[order[jnp.where(places < fixed, places, shifted)]].set(jnp.asarray(tallies, jnp.int32))

    tallies = jnp.where(number % 4 == 0, named(crowded, number // 4), named(usual, number - number // 4 - 1))
    mixed = jax.random.permutation(jax.random.fold_in(own, 3), number_of)
    giver, receiver = mixed[0:number_of // 2 * 2:2], mixed[1:number_of // 2 * 2:2]
    room = jnp.minimum(tallies[giver] - 1, limit - tallies[receiver]) // 2
    room = jnp.where((giver == order[0]) | (receiver == order[0]) | (tallies[receiver] == 0), 0, jnp.maximum(room, 0))
    shifted = jax.random.randint(jax.random.fold_in(own, 4), (number_of // 2,), 0, 1 << 20) % (room + 1)
    tallies = tallies.at[giver].add(-shifted).at[receiver].add(shifted)
    items = jnp.searchsorted(jnp.cumsum(tallies), jnp.arange(rows * top), side="right").astype(jnp.int32)
    listing = items.reshape(top, rows).T
    listing = listing[jax.random.permutation(jax.random.fold_in(own, 1), rows)]
    offset_by = jax.random.randint(jax.random.fold_in(own, 2), (rows, 1), 0, top)
    return jnp.take_along_axis(listing, (jnp.arange(top)[None, :] + offset_by) % top, axis=1)


def load_shares(count, total, most, skew, full):
    weights = [(1 << 20) // math.isqrt(grade ** skew) + 1 for grade in range(1, count + 1)]
    largest = most if full else min(most, max(-(-total // count), total * weights[0] // sum(weights)))
    least = 1 if total - largest >= count - 1 else 0
    holding, rest = [largest] + [least] * (count - 1), total - largest - least * (count - 1)
    while rest > 0:
        candidates = [i for i in range(1, count) if holding[i] < largest] or [i for i in range(1, count) if holding[i] < most]
        whole, budget = sum([weights[i] for i in candidates]), rest
        for i in candidates:
            extra = min(most - holding[i], max(1, budget * weights[i] // whole), rest)
            holding[i] = holding[i] + extra
            rest = rest - extra
    return np.array(holding)


def scatter_about(rng, dims, scale, most, pieces=(), held_as=jnp.bfloat16):
    gain = levels(rng, dims, pieces, -0.22, 0.18) if pieces else 1.0
    entries = jax.random.normal(rng, dims, jnp.float32) * scale * gain
    return jnp.minimum(jnp.maximum(entries, -most), most).astype(held_as)


def setup_inputs(seed: int = 0) -> dict:
    splits = jax.random.split(jax.random.key(seed), 10)
    texts = draw_texts(jax.random.fold_in(splits[9], 71), 0)
    qkv_weight = scatter_about(splits[1], (D, 3 * D), D ** -0.5, 0.21875, ((1, 64),))
    norm_gain = jnp.clip(1.0 + 0.18 * jax.random.normal(splits[2], (D,), jnp.float32), 0.1, 1.9)
    routes_keys = jax.random.split(jax.random.fold_in(splits[3], 1), TITLES // TITLES_DEV)
    routes_turns = jax.random.permutation(jax.random.fold_in(splits[3], 3), TITLES // TITLES_DEV)
    routes = jax.vmap(lambda own, number: assign_block(jax.random.fold_in(splits[3], 2), own, number, TITLES_DEV, N_DP, COPIES, CAP, 2))(routes_keys, routes_turns).reshape((TITLES, COPIES))
    w_self = scatter_about(splits[4], (D, HID), D ** -0.5, 0.21875, ((1, 8),), jnp.float32)
    w_neigh = scatter_about(splits[5], (D, HID), D ** -0.5, 0.21875, ((1, 8),), jnp.float32)
    gnn_bias = scatter_about(splits[6], (HID,), 0.5, 3.0, ((0, 8),), jnp.float32)
    neighbors = plant(jax.random.randint(splits[7], (N_DP * PART_ROWS, FAN), 0, PART_ROWS), jax.random.fold_in(splits[7], 1), 0, PART_ROWS - 1).astype(jnp.int32)
    cotangent = scatter_about(splits[8], (N_DP * PART_ROWS, HID), 1.0, 6.0, ((0, 64), (1, 8)), jnp.float32)
    return {"texts": texts, "qkv_weight": qkv_weight, "norm_gain": norm_gain, "routes": routes, "w_self": w_self, "w_neigh": w_neigh, "gnn_bias": gnn_bias, "neighbors": neighbors, "cotangent": cotangent}


def encode_block(block, qkv_weight, norm_gain):
    head_size = D // HEADS
    title_count = block.shape[0]
    flat_rows = block.reshape(title_count * SEQ, D)
    projected = jnp.dot(flat_rows, qkv_weight, preferred_element_type=jnp.float32).astype(jnp.bfloat16)
    projected = projected.reshape(title_count, SEQ, 3, HEADS, head_size)
    query = projected[:, :, 0].astype(jnp.float32)
    keys_part = projected[:, :, 1].astype(jnp.float32)
    values_part = projected[:, :, 2].astype(jnp.float32)
    scores = jnp.einsum('tqhd,tkhd->thqk', query, keys_part) / math.sqrt(head_size)
    probs = jax.nn.softmax(scores, axis=-1).astype(jnp.bfloat16)
    probs = lax.optimization_barrier(probs).astype(jnp.float32)
    attended = jnp.einsum('thqk,tkhd->tqhd', probs, values_part)
    pooled = lax.optimization_barrier(jnp.mean(attended, axis=1)).reshape(title_count, D)
    center = lax.optimization_barrier(jnp.mean(pooled, axis=1, keepdims=True))
    spread = lax.optimization_barrier(jnp.mean((pooled - center) ** 2, axis=1, keepdims=True))
    normed = (pooled - center) / jnp.sqrt(spread + 1e-05) * norm_gain
    return normed.astype(jnp.bfloat16)

def reference(texts, qkv_weight, norm_gain, routes, w_self, w_neigh, gnn_bias, neighbors, cotangent):
    block_total = N_DP * N_GRAPH
    blocks = texts.reshape(block_total, TITLES_DEV, SEQ, D)
    features = lax.map(lambda block: encode_block(block, qkv_weight, norm_gain), blocks)
    targets = routes.reshape(block_total, TITLES_DEV * COPIES)
    onehot = (targets[:, :, None] == jnp.arange(N_DP, dtype=jnp.int32)[None, None, :]).astype(jnp.int32)
    before = jnp.cumsum(onehot, axis=1) - onehot
    slot_rank = lax.optimization_barrier(jnp.sum(before * onehot, axis=2)).astype(jnp.int32)
    block_ids = jnp.arange(block_total, dtype=jnp.int32)
    source_dp = block_ids // N_GRAPH
    source_group = block_ids % N_GRAPH
    slots = source_group[:, None] * SLOTS + source_dp[:, None] * CAP + slot_rank
    copied = jnp.repeat(features, COPIES, axis=1).astype(jnp.float32).reshape(-1, D)
    flat_targets = targets.reshape(-1)
    flat_slots = slots.reshape(-1).astype(jnp.int32)
    part_rows = jnp.zeros((N_DP, PART_ROWS, D), jnp.float32).at[flat_targets, flat_slots].set(copied)

    def graph_layer(inputs):
        rows_in, neighbor_rows, cot_rows = inputs
        self_part = jnp.dot(rows_in, w_self, precision=lax.Precision.HIGHEST, preferred_element_type=jnp.float32)
        neigh_part = jnp.dot(rows_in, w_neigh, precision=lax.Precision.HIGHEST, preferred_element_type=jnp.float32)
        neighbor_sum = lax.optimization_barrier(jnp.sum(neigh_part[neighbor_rows], axis=1))
        preact = self_part + neighbor_sum + gnn_bias
        gate_sig = jax.nn.sigmoid(preact)
        hidden = preact * gate_sig
        pre_grad = cot_rows * gate_sig * (1.0 + preact * (1.0 - gate_sig))
        spread_grad = jnp.broadcast_to(pre_grad[:, None, :], (PART_ROWS, FAN, HID)).reshape(-1, HID)
        back = jax.ops.segment_sum(spread_grad, neighbor_rows.reshape(-1), num_segments=PART_ROWS)
        row_grads = jnp.dot(pre_grad, w_self.T, precision=lax.Precision.HIGHEST, preferred_element_type=jnp.float32)
        row_grads = row_grads + jnp.dot(back, w_neigh.T, precision=lax.Precision.HIGHEST, preferred_element_type=jnp.float32)
        return (hidden, row_grads)
    hidden_all, grads_all = lax.map(graph_layer, (part_rows, neighbors.reshape(N_DP, PART_ROWS, FAN), cotangent.reshape(N_DP, PART_ROWS, HID)))
    hidden_nodes = hidden_all.reshape(N_DP * PART_ROWS, HID)
    picked = grads_all[flat_targets, flat_slots].reshape(TITLES, COPIES, D)
    node_grads = lax.optimization_barrier(jnp.sum(picked, axis=1))
    return (hidden_nodes, node_grads)
```

```python
import functools

import jax
import jax.numpy as jnp
from jax import lax
from jax.experimental import pallas as pl
from jax.experimental.pallas import tpu as pltpu
from jax.sharding import PartitionSpec as P

NX, NZ, NC, NY = 4, 8, 2, 8
D = 768
HALF = 384
TITLES = 4
SEQ = 128
COLS = 256
ROWS = 1024
FAN = 15
BF16 = jnp.bfloat16
F32 = jnp.float32
NT = (((1,), (1,)), ((), ()))
NN = (((1,), (0,)), ((), ()))


def dot(a, b, dims=NN):
    return lax.dot_general(a, b, dims, preferred_element_type=F32)


def split(value):
    high = value.astype(BF16)
    return high, (value - high.astype(F32)).astype(BF16)


def iota(shape, axis):
    return lax.broadcasted_iota(jnp.int32, shape, axis)


def kernel(
    texts, wt, gain, routes, w_self, w_neigh, bias, near, cot,
    hidden_out, grads_out,
    wa, wb, dense, qkv, pooled, adj_t, adj, w_hi, w_lo,
    ry, rt, sel, sel_t, feats, tg, xs, ds, ub, ur, vs, vr, yo, yr, po, pr,
    sa_x, ra_x, sa_z, ra_z, sa_d, ra_d, sb_z, rb_z, sb_x, rb_x, sb_d, rb_d,
    sr_y, rr_y, sr_z, rr_z, sr_x, rr_x, sr_d, rr_d,
    sf, rf, st_z, rt_z, st_x, rt_x, st_d, rt_d,
    su_d, ru_d, su_x, ru_x, su_z, ru_z, sp, rp,
):
    dp = lax.axis_index("dp")
    y = lax.axis_index("graph")
    x = dp // 16
    z = (dp // 2) % 8
    c = dp % 2
    other = 1 - c

    def at(px, pz, pc, py):
        return (px * 16 + pz * 2 + pc, py)

    def xp(k):
        return at((x + k) % NX, z, c, y)

    def zp(k):
        return at(x, (z + k) % NZ, c, y)

    def yp(k):
        return at(x, z, c, (y + k) % NY)

    mate = at(x, z, other, y)

    def send(src, dst, ssem, rsem, peer):
        return pltpu.make_async_remote_copy(
            src_ref=src, dst_ref=dst, send_sem=ssem, recv_sem=rsem,
            device_id=peer, device_id_type=pl.DeviceIdType.MESH,
        )

    def loop(low, high, body):
        def step(i, carry):
            body(i)
            return carry
        lax.fori_loop(low, high, step, 0)

    def a_x(k):
        return send(wa.at[c, z, x], wa.at[c, z, x], sa_x.at[k], ra_x.at[k], xp(k))

    def a_z(step, way):
        hops = step if way == 0 else -step
        chunk = (z - hops + NZ) % NZ
        part = wa.at[c, chunk]
        if step == 3:
            part = part.at[pl.ds(2 * way, 2)]
        peer = zp(1) if way == 0 else zp(NZ - 1)
        return send(part, part, sa_z.at[step, way], ra_z.at[step, way], peer)

    def a_d(step, way):
        hops = step if way == 0 else -step
        chunk = (z - hops + NZ) % NZ
        part = wa.at[c, chunk]
        if step == 4:
            part = part.at[pl.ds(2 * way, 2)]
        return send(part, part, sa_d.at[step, way], ra_d.at[step, way], mate)

    def b_z(k):
        return send(wb.at[c, x, z], wb.at[c, x, z], sb_z.at[k], rb_z.at[k], zp(k))

    def b_x(k):
        return send(wb.at[c, x], wb.at[c, x], sb_x.at[k], rb_x.at[k], xp(k))

    def b_d(k):
        part = wb.at[c, (x - k + NX) % NX]
        return send(part, part, sb_d.at[k], rb_d.at[k], mate)

    def r_y(k):
        return send(ry.at[y], ry.at[y], sr_y.at[k], rr_y.at[k], yp(k))

    def r_z(k):
        return send(rt.at[x, c, z], rt.at[x, c, z], sr_z.at[k], rr_z.at[k], zp(k))

    def r_x(k):
        return send(rt.at[x, c], rt.at[x, c], sr_x.at[k], rr_x.at[k], xp(k))

    def r_d(k):
        part = rt.at[(x - k + NX) % NX, c]
        return send(part, part, sr_d.at[k], rr_d.at[k], mate)

    def f_y(k):
        return send(feats.at[y], feats.at[y], sf.at[k], rf.at[k], yp(k))

    def t_z(k):
        return send(tg.at[x, c, z], tg.at[x, c, z], st_z.at[k], rt_z.at[k], zp(k))

    def t_x(k):
        return send(tg.at[x, c], tg.at[x, c], st_x.at[k], rt_x.at[k], xp(k))

    def t_d(k):
        part = tg.at[(x - k + NX) % NX, c]
        return send(part, part, st_d.at[k], rt_d.at[k], mate)

    def u_d(k):
        to = (x + k) % NX
        return send(ub.at[to, other], ur.at[to], su_d.at[k], ru_d.at[k], mate)

    def u_x(k):
        return send(vs.at[(x + k) % NX], vr.at[k], su_x.at[k], ru_x.at[k], xp(k))

    def u_z(k):
        return send(yo.at[(z + k) % NZ], yr.at[k], su_z.at[k], ru_z.at[k], zp(k))

    def p_y(k):
        return send(po.at[(y + k) % NY], pr.at[k], sp.at[k], rp.at[k], yp(k))

    barrier = pltpu.get_barrier_semaphore()

    def greet(peer):
        pl.semaphore_signal(barrier, inc=1, device_id=peer, device_id_type=pl.DeviceIdType.MESH)

    greet(mate)
    loop(1, NX, lambda k: greet(xp(k)))
    loop(1, NZ, lambda k: greet(zp(k)))
    loop(1, NY, lambda k: greet(yp(k)))

    wa[c, z, x] = wt[:, :HALF]
    wb[c, x, z] = wt[:, HALF:]
    lane = iota((8, 128), 1)
    row = iota((8, 128), 0)
    spread = ((iota((8, 128), 1) % 8) == iota((8, 128), 0)).astype(BF16)
    tiled = dot(routes[...].astype(F32).astype(BF16), spread)
    own = jnp.sum(jnp.where((iota((TITLES, 128), 1) // 8) == iota((TITLES, 128), 0), tiled, 0.0), axis=0, keepdims=True)
    ry[y] = jnp.where(row == y, jnp.broadcast_to(own, (8, 128)), 0.0)

    pl.semaphore_wait(barrier, 1 + (NX - 1) + (NZ - 1) + (NY - 1))

    loop(1, NX, lambda k: a_x(k).start())
    loop(1, NY, lambda k: r_y(k).start())
    loop(1, NZ, lambda k: b_z(k).start())

    def count(first, last):
        def body(step):
            j0 = pl.multiple_of((step // 4) * 64, 64)
            i0 = pl.multiple_of((step % 4) * 256, 256)
            rows = iota((64, 256), 0) + j0
            total = jnp.zeros((64, 256), F32)
            for k in range(FAN):
                total = total + jnp.where(rows == near[k:k + 1, pl.ds(i0, 256)], 1.0, 0.0)
            adj_t[pl.ds(j0, 64), pl.ds(i0, 256)] = total.astype(BF16)
        loop(first, last, body)

    def flip(step):
        r0 = pl.multiple_of((step // 4) * 256, 256)
        c0 = pl.multiple_of((step % 4) * 256, 256)
        adj[pl.ds(r0, 256), pl.ds(c0, 256)] = adj_t[pl.ds(c0, 256), pl.ds(r0, 256)].astype(F32).T.astype(BF16)

    count(0, 12)
    loop(1, NX, lambda k: a_x(k).wait_recv())
    a_z(0, 0).start()
    a_z(0, 1).start()
    a_d(0, 0).start()
    loop(1, NY, lambda k: r_y(k).wait_recv())
    rt[x, c, z] = jnp.sum(ry[...], axis=0)
    loop(1, NZ, lambda k: r_z(k).start())
    count(12, 24)
    loop(1, NZ, lambda k: b_z(k).wait_recv())
    loop(1, NX, lambda k: b_x(k).start())
    b_d(0).start()
    a_z(0, 0).wait_recv()
    a_z(0, 1).wait_recv()
    a_z(1, 0).start()
    a_z(1, 1).start()
    a_d(1, 0).start()
    a_d(1, 1).start()
    loop(1, NZ, lambda k: r_z(k).wait_recv())
    loop(1, NX, lambda k: r_x(k).start())
    r_d(0).start()
    count(24, 40)
    a_z(1, 0).wait_recv()
    a_z(1, 1).wait_recv()
    a_z(2, 0).start()
    a_z(2, 1).start()
    a_d(2, 0).start()
    a_d(2, 1).start()
    loop(1, NX, lambda k: r_x(k).wait_recv())
    loop(1, NX, lambda k: r_d(k).start())
    count(40, 56)
    a_z(2, 0).wait_recv()
    a_z(2, 1).wait_recv()
    a_z(3, 0).start()
    a_z(3, 1).start()
    a_d(3, 0).start()
    a_d(3, 1).start()
    count(56, 64)
    loop(0, 16, flip)
    w_hi[:, :128], w_lo[:, :128] = split(w_self[...])
    w_hi[:, 128:], w_lo[:, 128:] = split(w_neigh[...])

    loop(0, NX, lambda k: r_d(k).wait_recv())
    title = iota((128, 512), 1)
    named = iota((128, 512), 0)
    same = jnp.where((named < 32) & (named // 8 == title % 4), 1.0, 0.0).astype(BF16)
    ahead = jnp.where((named < 32) & (named // 8 < title % 4), 1.0, 0.0).astype(BF16)
    mine = (title // 4) == named
    slot = iota((256, 512), 0)
    col = iota((256, 512), 1)
    match = (
        (slot // 32 == (col % 32) // 4)
        & ((slot % 32) // 4 == (col % 256) // 32)
        & ((slot % 4) // 2 == col // 256)
    )
    wanted = jnp.where(match, (slot % 2).astype(F32) + 1.0, -1.0)

    def select(block):
        listed = rt[block].reshape(128, 128)
        hits = jnp.where(listed == dp.astype(F32), 1.0, 0.0).astype(BF16)
        code = dot(hits, same) * (1.0 + dot(hits, ahead))
        code = jnp.sum(jnp.where(mine, code, 0.0), axis=0, keepdims=True)
        chosen = jnp.where(code == wanted, 1.0, 0.0)
        sel[block] = chosen.astype(BF16)
        sel_t[block] = chosen.T.astype(BF16)

    loop(0, NX, select)

    loop(1, NX, lambda k: b_x(k).wait_recv())
    loop(1, NX, lambda k: b_d(k).start())
    a_z(3, 0).wait_recv()
    a_z(3, 1).wait_recv()
    a_d(4, 0).start()
    a_d(4, 1).start()
    loop(0, NX, lambda k: b_d(k).wait_recv())
    a_d(0, 0).wait_recv()
    for step in range(1, 5):
        a_d(step, 0).wait_recv()
        a_d(step, 1).wait_recv()

    def pack(group):
        gx = group // 4
        gz = (group % 4) * 2
        base = pl.multiple_of(group * 144, 16)
        left = [wa[cc, gz + dz, gx].astype(F32) for dz in range(2) for cc in range(2)]
        right = [wb[cc, gx, gz + dz].astype(F32) for dz in range(2) for cc in range(2)]
        dense[pl.ds(base, 144), :HALF] = jnp.concatenate(left, axis=0).astype(BF16)
        dense[pl.ds(base, 144), HALF:] = jnp.concatenate(right, axis=0).astype(BF16)

    loop(0, 16, pack)

    def project(block):
        rows = dense[pl.ds(pl.multiple_of(block * 256, 256), 256), :]
        qkv[block] = dot(texts[...], rows, NT).astype(BF16).reshape(TITLES, SEQ, 256)

    loop(0, 9, project)

    head = iota((SEQ, 256), 1) // 64

    def attend(step):
        block = step // TITLES
        title_at = step % TITLES
        q = qkv[block, title_at]
        k = qkv[3 + block, title_at]
        v = qkv[6 + block, title_at]
        zero = jnp.zeros_like(k)
        keys = jnp.concatenate([jnp.where(head == h, k, zero) for h in range(4)], axis=0)
        vals = jnp.concatenate([jnp.where(head == h, v, zero) for h in range(4)], axis=0)
        scores = dot(q, keys, NT) * 0.125
        weights = []
        for h in range(4):
            part = scores[:, h * SEQ:(h + 1) * SEQ]
            part = jnp.exp(part - jnp.max(part, axis=1, keepdims=True))
            part = part / jnp.sum(part, axis=1, keepdims=True)
            weights.append(jnp.sum(part.astype(BF16).astype(F32), axis=0, keepdims=True))
        high, low = split(jnp.broadcast_to(jnp.concatenate(weights, axis=1), (8, 512)))
        pooled[step] = (dot(high, vals) + dot(low, vals)) * (1.0 / SEQ)

    loop(0, 3 * TITLES, attend)

    means = jnp.concatenate(
        [
            jnp.concatenate([pooled[b * TITLES + t][0:1] for b in range(3)], axis=1)
            for t in range(TITLES)
        ],
        axis=0,
    )
    center = jnp.mean(means, axis=1, keepdims=True)
    variance = jnp.mean((means - center) ** 2, axis=1, keepdims=True)
    feats[y] = ((means - center) / jnp.sqrt(variance + 1e-05) * gain[...]).astype(BF16)

    loop(1, NY, lambda k: f_y(k).start())
    loop(1, NY, lambda k: f_y(k).wait_recv())
    group_feats = jnp.concatenate([feats[g].astype(F32) for g in range(NY)], axis=0).astype(BF16)
    tg[x, c, z] = (dot(group_feats, w_hi[...]) + dot(group_feats, w_lo[...])).astype(BF16)

    loop(1, NZ, lambda k: t_z(k).start())
    loop(1, NZ, lambda k: t_z(k).wait_recv())
    loop(1, NX, lambda k: t_x(k).start())
    t_d(0).start()

    def place(block):
        rows = dot(sel[block], tg[block].reshape(512, COLS)).astype(BF16)
        for g in range(NY):
            xs[pl.ds(pl.multiple_of(g * 128 + block * 32, 32), 32), :] = rows[g * 32:(g + 1) * 32]

    t_d(0).wait_recv()
    place(x)
    for k in range(1, NX):
        t_x(k).wait_recv()
        t_d(k).start()
    for k in range(1, NX):
        t_d(k).wait_recv()
        place((x - k + NX) % NX)

    def layer(step):
        rows = pl.ds(pl.multiple_of(step * 256, 256), 256)
        total = xs[rows, :128].astype(F32) + dot(adj[rows, :], xs[:, 128:]) + bias[...]
        gate = 1.0 / (1.0 + jnp.exp(-total))
        hidden_out[rows, :] = total * gate
        ds[rows, :128] = (cot[rows, :] * gate * (1.0 + total * (1.0 - gate))).astype(BF16)

    loop(0, 4, layer)

    def backward(step):
        rows = pl.ds(pl.multiple_of(step * 256, 256), 256)
        ds[rows, 128:] = dot(adj_t[rows, :], ds[:, :128]).astype(BF16)

    loop(0, 4, backward)

    def titles_of(block):
        rows = jnp.concatenate(
            [ds[pl.ds(pl.multiple_of(g * 128 + block * 32, 32), 32), :] for g in range(NY)], axis=0
        )
        ub[block] = dot(sel_t[block], rows).astype(BF16).reshape(NC, 256, COLS)

    for k in (1, 2, 3, 0):
        titles_of((x + k) % NX)
        u_d(k).start()
    for k in (1, 2, 3, 0):
        to = (x + k) % NX
        u_d(k).wait_recv()
        vs[to] = (ub[to, c].astype(F32) + ur[to].astype(F32)).astype(BF16)
        if k:
            u_x(k).start()
    total = vs[x].astype(F32)
    for k in range(1, NX):
        u_x(k).wait_recv()
        total = total + vr[k].astype(F32)
    yo[...] = total.astype(BF16).reshape(NZ, 32, COLS)
    loop(1, NZ, lambda k: u_z(k).start())
    node = yo[z].astype(F32)
    for k in range(1, NZ):
        u_z(k).wait_recv()
        node = node + yr[k].astype(F32)
    high, low = split(node)
    partial = dot(high, w_hi[...], NT) + dot(high, w_lo[...], NT) + dot(low, w_hi[...], NT)
    for g in range(NY):
        po[g] = partial[g * 4:(g + 1) * 4].astype(BF16)
    loop(1, NY, lambda k: p_y(k).start())
    result = po[y].astype(F32)
    for k in range(1, NY):
        p_y(k).wait_recv()
        result = result + pr[k].astype(F32)
    grads_out[...] = result

    loop(1, NX, lambda k: a_x(k).wait_send())
    loop(1, NX, lambda k: b_x(k).wait_send())
    loop(1, NX, lambda k: r_x(k).wait_send())
    loop(1, NX, lambda k: t_x(k).wait_send())
    loop(1, NX, lambda k: u_x(k).wait_send())
    loop(1, NZ, lambda k: b_z(k).wait_send())
    loop(1, NZ, lambda k: r_z(k).wait_send())
    loop(1, NZ, lambda k: t_z(k).wait_send())
    loop(1, NZ, lambda k: u_z(k).wait_send())
    loop(1, NY, lambda k: r_y(k).wait_send())
    loop(1, NY, lambda k: f_y(k).wait_send())
    loop(1, NY, lambda k: p_y(k).wait_send())
    loop(0, NX, lambda k: b_d(k).wait_send())
    loop(0, NX, lambda k: r_d(k).wait_send())
    loop(0, NX, lambda k: t_d(k).wait_send())
    loop(0, NX, lambda k: u_d(k).wait_send())
    for step in range(4):
        a_z(step, 0).wait_send()
        a_z(step, 1).wait_send()
    a_d(0, 0).wait_send()
    for step in range(1, 5):
        a_d(step, 0).wait_send()
        a_d(step, 1).wait_send()


def shards(texts, qkv_weight, norm_gain, routes, w_self, w_neigh, gnn_bias, neighbors, cotangent):
    vmem = pl.BlockSpec(memory_space=pltpu.VMEM)
    dma = pltpu.SemaphoreType.DMA
    hidden, grads = pl.pallas_call(
        kernel,
        out_shape=(
            jax.ShapeDtypeStruct((ROWS, 128), F32),
            jax.ShapeDtypeStruct((TITLES, D), F32),
        ),
        in_specs=[vmem] * 9,
        out_specs=(vmem, vmem),
        scratch_shapes=[
            pltpu.VMEM((NC, NZ, NX, 36, HALF), BF16),
            pltpu.VMEM((NC, NX, NZ, 36, HALF), BF16),
            pltpu.VMEM((3 * D, D), BF16),
            pltpu.VMEM((9, TITLES, SEQ, 256), BF16),
            pltpu.VMEM((12, 8, 256), F32),
            pltpu.VMEM((ROWS, ROWS), BF16),
            pltpu.VMEM((ROWS, ROWS), BF16),
            pltpu.VMEM((D, COLS), BF16),
            pltpu.VMEM((D, COLS), BF16),
            pltpu.VMEM((NY, 8, 128), F32),
            pltpu.VMEM((NX, NC, NZ, 8, 128), F32),
            pltpu.VMEM((NX, 256, 512), BF16),
            pltpu.VMEM((NX, 512, 256), BF16),
            pltpu.VMEM((NY, TITLES, D), BF16),
            pltpu.VMEM((NX, NC, NZ, 32, COLS), BF16),
            pltpu.VMEM((ROWS, COLS), BF16),
            pltpu.VMEM((ROWS, COLS), BF16),
            pltpu.VMEM((NX, NC, 256, COLS), BF16),
            pltpu.VMEM((NX, 256, COLS), BF16),
            pltpu.VMEM((NX, 256, COLS), BF16),
            pltpu.VMEM((NX, 256, COLS), BF16),
            pltpu.VMEM((NZ, 32, COLS), BF16),
            pltpu.VMEM((NZ, 32, COLS), BF16),
            pltpu.VMEM((NY, TITLES, D), BF16),
            pltpu.VMEM((NY, TITLES, D), BF16),
            dma((NX,)), dma((NX,)),
            dma((4, 2)), dma((4, 2)),
            dma((5, 2)), dma((5, 2)),
            dma((NZ,)), dma((NZ,)),
            dma((NX,)), dma((NX,)),
            dma((NX,)), dma((NX,)),
            dma((NY,)), dma((NY,)),
            dma((NZ,)), dma((NZ,)),
            dma((NX,)), dma((NX,)),
            dma((NX,)), dma((NX,)),
            dma((NY,)), dma((NY,)),
            dma((NZ,)), dma((NZ,)),
            dma((NX,)), dma((NX,)),
            dma((NX,)), dma((NX,)),
            dma((NX,)), dma((NX,)),
            dma((NX,)), dma((NX,)),
            dma((NZ,)), dma((NZ,)),
            dma((NY,)), dma((NY,)),
        ],
        compiler_params=pltpu.CompilerParams(
            collective_id=0, has_side_effects=True, vmem_limit_bytes=48 * 2**20
        ),
        name="glem_step",
    )(
        texts.reshape(TITLES * SEQ, D),
        qkv_weight.T,
        norm_gain.reshape(1, D),
        routes,
        w_self,
        w_neigh,
        gnn_bias.reshape(1, 128),
        neighbors.T,
        cotangent,
    )
    return hidden, grads


def solution(mesh):
    placed = (
        P(("dp", "graph"), None, None),
        P(None, "dp"),
        P(),
        P(("dp", "graph"), None),
        P(None, "graph"),
        P(None, "graph"),
        P("graph"),
        P("dp", None),
        P("dp", "graph"),
    )
    return jax.shard_map(
        shards,
        mesh=mesh,
        in_specs=placed,
        out_specs=(P("dp", "graph"), P(("dp", "graph"), None)),
        check_vma=False,
    )
```

```python
import functools

import jax
import jax.numpy as jnp
from jax import lax
from jax.experimental import pallas as pl
from jax.experimental.pallas import tpu as pltpu
from jax.sharding import PartitionSpec as P

NX, NZ, NC, NY = 4, 8, 2, 8
D = 768
HALF = 384
WIDE = 36
PIECE = 112
TITLES = 4
SEQ = 128
COLS = 256
ROWS = 1024
FAN = 15
BF16 = jnp.bfloat16
F32 = jnp.float32
NT = (((1,), (1,)), ((), ()))
NN = (((1,), (0,)), ((), ()))


def dot(a, b, dims=NN):
    return lax.dot_general(a, b, dims, preferred_element_type=F32)


def split(value):
    high = value.astype(BF16)
    return high, (value - high.astype(F32)).astype(BF16)


def iota(shape, axis):
    return lax.broadcasted_iota(jnp.int32, shape, axis)


def kernel(
    texts_in, wt_in, gain_in, routes_in, w_self_in, w_neigh_in, bias_in, near_in, cot_in,
    hidden_out, grads_out,
    texts, wt, gain, routes, w_self, w_neigh, bias, near, cot, load,
    wa, wb, dense, qt, keys, vals, pooled, adj_t, adj, w_hi, w_lo,
    ry, rt, sel, sel_t, feats, tg, xs, ds, ub, ur, vs, vr, yo, yr, po, pr,
    sa_x, ra_x, sa_z, ra_z, sa_d, ra_d, sb_z, rb_z, sb_x, rb_x, sb_d, rb_d,
    sr_y, rr_y, sr_z, rr_z, sr_x, rr_x, sr_d, rr_d,
    sf, rf, st_z, rt_z, st_x, rt_x, st_d, rt_d,
    su_d, ru_d, su_x, ru_x, su_z, ru_z, sp, rp,
):
    dp = lax.axis_index("dp")
    y = lax.axis_index("graph")
    x = dp // 16
    z = (dp // 2) % 8
    c = dp % 2
    other = 1 - c

    def at(px, pz, pc, py):
        return (px * 16 + pz * 2 + pc, py)

    def xp(k):
        return at((x + k) % NX, z, c, y)

    def zp(k):
        return at(x, (z + k) % NZ, c, y)

    def yp(k):
        return at(x, z, c, (y + k) % NY)

    mate = at(x, z, other, y)

    def send(src, dst, ssem, rsem, peer):
        return pltpu.make_async_remote_copy(
            src_ref=src, dst_ref=dst, send_sem=ssem, recv_sem=rsem,
            device_id=peer, device_id_type=pl.DeviceIdType.MESH,
        )

    def loop(low, high, body):
        def step(i, carry):
            body(i)
            return carry
        lax.fori_loop(low, high, step, 0)

    barrier = pltpu.get_barrier_semaphore()

    def greet(peer):
        pl.semaphore_signal(barrier, inc=1, device_id=peer, device_id_type=pl.DeviceIdType.MESH)

    greet(mate)
    loop(1, NX, lambda k: greet(xp(k)))
    loop(1, NZ, lambda k: greet(zp(k)))
    loop(1, NY, lambda k: greet(yp(k)))

    held = (texts, wt, gain, routes, w_self, w_neigh, bias, near, cot)
    given = (texts_in, wt_in, gain_in, routes_in, w_self_in, w_neigh_in, bias_in, near_in, cot_in)
    loads = [pltpu.make_async_copy(given[i], held[i], load.at[i]) for i in range(9)]
    for i in (1, 3, 7, 4, 5, 0, 2, 6, 8):
        loads[i].start()

    def a_x(k):
        return send(wa.at[c, z, x], wa.at[c, z, x], sa_x.at[k], ra_x.at[k], xp(k))

    def ring(step, way, sub):
        hops = step if way == 0 else -step
        return wa.at[c, (z - hops + NZ) % NZ, pl.ds(2 * sub, 2)]

    def a_z(step, way, sub):
        part = ring(step, way, sub)
        peer = zp(1) if way == 0 else zp(NZ - 1)
        return send(part, part, sa_z.at[step, way, sub], ra_z.at[step, way, sub], peer)

    def a_d(step, way, sub):
        part = ring(step, way, sub)
        return send(part, part, sa_d.at[step, way, sub], ra_d.at[step, way, sub], mate)

    def b_z(k):
        return send(wb.at[c, x, z], wb.at[c, x, z], sb_z.at[k], rb_z.at[k], zp(k))

    def b_x(k):
        return send(wb.at[c, x], wb.at[c, x], sb_x.at[k], rb_x.at[k], xp(k))

    def b_s(k, dz):
        part = wb.at[c, x, (z + dz) % NZ]
        return send(part, part, sb_x.at[k], rb_x.at[k], xp(k))

    def b_d(k):
        part = wb.at[c, (x - k + NX) % NX]
        return send(part, part, sb_d.at[k], rb_d.at[k], mate)

    def r_y(k):
        return send(ry.at[y], ry.at[y], sr_y.at[k], rr_y.at[k], yp(k))

    def r_z(k):
        return send(rt.at[x, c, z], rt.at[x, c, z], sr_z.at[k], rr_z.at[k], zp(k))

    def r_x(k):
        return send(rt.at[x, c], rt.at[x, c], sr_x.at[k], rr_x.at[k], xp(k))

    def r_d(k):
        part = rt.at[(x - k + NX) % NX, c]
        return send(part, part, sr_d.at[k], rr_d.at[k], mate)

    def f_y(k):
        return send(feats.at[y], feats.at[y], sf.at[k], rf.at[k], yp(k))

    def t_z(k):
        return send(tg.at[x, c, z], tg.at[x, c, z], st_z.at[k], rt_z.at[k], zp(k))

    def t_x(k):
        return send(tg.at[x, c], tg.at[x, c], st_x.at[k], rt_x.at[k], xp(k))

    def t_s(k, dz):
        part = tg.at[x, c, (z + dz) % NZ]
        return send(part, part, st_x.at[k], rt_x.at[k], xp(k))

    def t_d(k):
        part = tg.at[(x - k + NX) % NX, c]
        return send(part, part, st_d.at[k], rt_d.at[k], mate)

    def u_d(k):
        to = (x + k) % NX
        return send(ub.at[to, other], ur.at[to], su_d.at[k], ru_d.at[k], mate)

    def u_x(k, dz):
        to = (z + dz) % NZ
        return send(vs.at[(x + k) % NX, to], vr.at[k, dz], su_x.at[k, dz], ru_x.at[k, dz], xp(k))

    def u_z(k):
        return send(yo.at[k], yr.at[k], su_z.at[k], ru_z.at[k], zp(k))

    def p_y(k):
        return send(po.at[(y + k) % NY], pr.at[k], sp.at[k], rp.at[k], yp(k))

    loads[1].wait()
    shard = wt[...].astype(F32)
    filling = jnp.zeros((PIECE - 3 * WIDE, 128), F32)
    tiles = [shard[:, i * 128:(i + 1) * 128] for i in range(6)]
    wa[c, z, x] = jnp.concatenate(tiles[:3] + [filling], axis=0).astype(BF16)
    wb[c, x, z] = jnp.concatenate(tiles[3:] + [filling], axis=0).astype(BF16)
    loads[3].wait()
    row = iota((8, 128), 0)
    spread = ((iota((8, 128), 1) % 8) == iota((8, 128), 0)).astype(BF16)
    tiled = dot(routes[...].astype(F32).astype(BF16), spread)
    own = jnp.sum(jnp.where((iota((TITLES, 128), 1) // 8) == iota((TITLES, 128), 0), tiled, 0.0), axis=0, keepdims=True)
    ry[y] = jnp.where(row == y, jnp.broadcast_to(own, (8, 128)), 0.0)

    pl.semaphore_wait(barrier, 1 + (NX - 1) + (NZ - 1) + (NY - 1))

    loop(1, NX, lambda k: a_x(k).start())
    for k in (1, 7, 2, 6, 3, 5, 4):
        b_z(k).start()
    loop(1, NX, lambda k: b_s(k, 0).start())
    loop(1, NY, lambda k: r_y(k).start())

    def count(first, last):
        def body(step):
            j0 = pl.multiple_of((step // 4) * 64, 64)
            i0 = pl.multiple_of((step % 4) * 256, 256)
            rows = iota((64, 256), 0) + j0
            total = jnp.zeros((64, 256), F32)
            for k in range(FAN):
                total = total + jnp.where(rows == near[k:k + 1, pl.ds(i0, 256)], 1.0, 0.0)
            adj_t[pl.ds(j0, 64), pl.ds(i0, 256)] = total.astype(BF16)
        loop(first, last, body)

    def flip(step):
        r0 = pl.multiple_of((step // 4) * 256, 256)
        c0 = pl.multiple_of((step % 4) * 256, 256)
        adj[pl.ds(r0, 256), pl.ds(c0, 256)] = adj_t[pl.ds(c0, 256), pl.ds(r0, 256)].astype(F32).T.astype(BF16)

    def pass_b(k):
        b_z(k).wait_recv()
        loop(1, NX, lambda n: b_s(n, NZ - k).start())

    def pass_a(step):
        for way in range(2):
            for sub in range(2):
                a_z(step, way, sub).wait_recv()
                if step < 2 or way == sub:
                    a_z(step + 1, way, sub).start()
                a_d(step + 1, way, sub).start()

    loads[7].wait()
    count(0, 24)
    loop(1, NX, lambda k: a_x(k).wait_recv())
    for sub in range(2):
        for way in range(2):
            a_z(0, way, sub).start()
    a_d(0, 0, 0).start()
    a_d(0, 0, 1).start()
    pass_b(1)
    pass_b(7)
    count(24, 32)
    pass_b(2)
    pass_b(6)
    loop(1, NY, lambda k: r_y(k).wait_recv())
    rt[x, c, z] = jnp.sum(ry[...], axis=0)
    loop(1, NZ, lambda k: r_z(k).start())
    pass_a(0)
    pass_b(3)
    pass_b(5)
    pass_b(4)
    b_d(0).start()
    count(32, 44)
    pass_a(1)
    loop(1, NZ, lambda k: r_z(k).wait_recv())
    loop(1, NX, lambda k: r_x(k).start())
    r_d(0).start()
    count(44, 56)
    pass_a(2)
    loop(1, NX, lambda k: r_x(k).wait_recv())
    loop(1, NX, lambda k: r_d(k).start())
    count(56, 64)
    loads[4].wait()
    loads[5].wait()
    w_hi[:, :128], w_lo[:, :128] = split(w_self[...])
    w_hi[:, 128:], w_lo[:, 128:] = split(w_neigh[...])

    for k in (1, 3, 2):
        b_x(k).wait_recv()
        b_d(k).start()
    a_z(3, 0, 0).wait_recv()
    a_d(4, 0, 0).start()
    a_z(3, 1, 1).wait_recv()
    a_d(4, 1, 1).start()
    a_d(0, 0, 0).wait_recv()
    a_d(0, 0, 1).wait_recv()
    for step in range(1, 4):
        for way in range(2):
            for sub in range(2):
                a_d(step, way, sub).wait_recv()
    loop(0, NX, lambda k: b_d(k).wait_recv())
    a_d(4, 0, 0).wait_recv()
    a_d(4, 1, 1).wait_recv()
    loads[0].wait()
    loads[2].wait()
    loads[6].wait()
    loads[8].wait()

    def pack(group):
        gx = group // 4
        gz = (group % 4) * 2
        base = pl.multiple_of(group * 144, 16)
        left = [wa[cc, gz + dz, gx].astype(F32) for dz in range(2) for cc in range(2)]
        right = [wb[cc, gx, gz + dz].astype(F32) for dz in range(2) for cc in range(2)]
        for i in range(3):
            rows = slice(i * WIDE, (i + 1) * WIDE)
            for start, pieces in ((0, left), (HALF, right)):
                column = jnp.concatenate([piece[rows] for piece in pieces], axis=0)
                dense[pl.ds(base, 144), start + i * 128:start + (i + 1) * 128] = column.astype(BF16)

    loop(0, 16, pack)

    def project(block):
        at0 = pl.multiple_of(block * 256, 256)
        rows = pl.ds(at0, 256)
        title_q = dot(dense[rows, :], texts[...], NT).astype(BF16)
        for t in range(TITLES):
            qt[block, t] = title_q[:, t * SEQ:(t + 1) * SEQ]
        rows = pl.ds(pl.multiple_of(at0 + D, 256), 256)
        keys[block] = dot(texts[...], dense[rows, :], NT).astype(BF16).reshape(TITLES, SEQ, 256)
        rows = pl.ds(pl.multiple_of(at0 + 2 * D, 256), 256)
        vals[block] = dot(texts[...], dense[rows, :], NT).astype(BF16).reshape(TITLES, SEQ, 256)

    loop(0, 3, project)

    adder = jnp.where((iota((8, 4 * SEQ), 1) // SEQ) == (iota((8, 4 * SEQ), 0) % 4), 1.0, 0.0).astype(BF16)
    upper = iota((8, SEQ), 0) < 4
    own_head = (iota((8, 256), 1) // 64) == (iota((8, 256), 0) % 4)
    blank = jnp.zeros((64, SEQ), BF16)

    def attend(block):
        each = range(TITLES)
        scores = []
        for t in each:
            q = qt[block, t]
            queries = jnp.concatenate(
                [
                    jnp.concatenate([q[h * 64:(h + 1) * 64] if i == h else blank for i in range(4)], axis=1)
                    for h in range(4)
                ],
                axis=0,
            )
            scores.append(dot(keys[block, t], queries) * 0.125)
        scores = [jnp.exp(s - jnp.max(s, axis=0, keepdims=True)) for s in scores]
        probs = [(s * (1.0 / jnp.sum(s, axis=0, keepdims=True))).astype(BF16) for s in scores]
        sums = [split(dot(adder, p, NT)) for p in probs]
        sums = [jnp.where(upper, high.astype(F32), low.astype(F32)).astype(BF16) for high, low in sums]
        mixed = [dot(sums[t], vals[block, t]) for t in each]
        for t in each:
            row = jnp.sum(jnp.where(own_head, mixed[t], 0.0), axis=0, keepdims=True) * (1.0 / SEQ)
            pooled[block * TITLES + t] = jnp.broadcast_to(row, (8, 256))

    loop(0, 3, attend)

    means = jnp.concatenate(
        [
            jnp.concatenate([pooled[b * TITLES + t][0:1] for b in range(3)], axis=1)
            for t in range(TITLES)
        ],
        axis=0,
    )
    center = jnp.mean(means, axis=1, keepdims=True)
    variance = jnp.mean((means - center) ** 2, axis=1, keepdims=True)
    feats[y] = ((means - center) / jnp.sqrt(variance + 1e-05) * gain[...]).astype(BF16)

    loop(1, NY, lambda k: f_y(k).start())
    loop(0, NX, lambda k: r_d(k).wait_recv())
    title = iota((128, 512), 1)
    named = iota((128, 512), 0)
    same = jnp.where((named < 32) & (named // 8 == title % 4), 1.0, 0.0).astype(BF16)
    ahead = jnp.where((named < 32) & (named // 8 < title % 4), 1.0, 0.0).astype(BF16)
    mine = (title // 4) == named
    slot = iota((256, 512), 0)
    col = iota((256, 512), 1)
    match = (
        (slot // 32 == (col % 32) // 4)
        & ((slot % 32) // 4 == (col % 256) // 32)
        & ((slot % 4) // 2 == col // 256)
    )
    wanted = jnp.where(match, (slot % 2).astype(F32) + 1.0, -1.0)

    def select(block):
        listed = rt[block].reshape(128, 128)
        hits = jnp.where(listed == dp.astype(F32), 1.0, 0.0).astype(BF16)
        code = dot(hits, same) * (1.0 + dot(hits, ahead))
        code = jnp.sum(jnp.where(mine, code, 0.0), axis=0, keepdims=True)
        chosen = jnp.where(code == wanted, 1.0, 0.0)
        sel[block] = chosen.astype(BF16)
        sel_t[block] = chosen.T.astype(BF16)

    loop(0, NX, select)

    loop(1, NY, lambda k: f_y(k).wait_recv())
    group_feats = jnp.concatenate([feats[g].astype(F32) for g in range(NY)], axis=0).astype(BF16)
    tg[x, c, z] = (dot(group_feats, w_hi[...]) + dot(group_feats, w_lo[...])).astype(BF16)

    for k in (1, 7, 2, 6, 3, 5, 4):
        t_z(k).start()
    loop(1, NX, lambda k: t_s(k, 0).start())
    loop(0, 16, flip)
    for k in (1, 7, 2, 6, 3, 5, 4):
        t_z(k).wait_recv()
        loop(1, NX, lambda n: t_s(n, NZ - k).start())
    t_d(0).start()

    def place(block):
        rows = dot(sel[block], tg[block].reshape(512, COLS)).astype(BF16)
        for g in range(NY):
            xs[pl.ds(pl.multiple_of(g * 128 + block * 32, 32), 32), :] = rows[g * 32:(g + 1) * 32]

    t_d(0).wait_recv()
    place(x)
    for k in (1, 3, 2):
        t_x(k).wait_recv()
        t_d(k).start()
    for k in (1, 3, 2):
        t_d(k).wait_recv()
        place((x - k + NX) % NX)

    def layer(step):
        rows = pl.ds(pl.multiple_of(step * 256, 256), 256)
        total = xs[rows, :128].astype(F32) + dot(adj[rows, :], xs[:, 128:]) + bias[...]
        gate = 1.0 / (1.0 + jnp.exp(-total))
        hidden_out[rows, :] = total * gate
        ds[rows, :128] = (cot[rows, :] * gate * (1.0 + total * (1.0 - gate))).astype(BF16)

    loop(0, 4, layer)

    def backward(step):
        rows = pl.ds(pl.multiple_of(step * 256, 256), 256)
        ds[rows, 128:] = dot(adj_t[rows, :], ds[:, :128]).astype(BF16)

    loop(0, 4, backward)

    def titles_of(block):
        rows = jnp.concatenate(
            [ds[pl.ds(pl.multiple_of(g * 128 + block * 32, 32), 32), :] for g in range(NY)], axis=0
        )
        ub[block] = dot(sel_t[block], rows).astype(BF16).reshape(NC, 256, COLS)

    for k in (1, 2, 3, 0):
        titles_of((x + k) % NX)
        u_d(k).start()
    for k in (1, 2, 3):
        to = (x + k) % NX
        u_d(k).wait_recv()
        vs[to] = (ub[to, c].astype(F32) + ur[to].astype(F32)).astype(BF16).reshape(NZ, 32, COLS)
        loop(0, NZ, lambda dz: u_x(k, (dz + 4) % NZ).start())
    u_d(0).wait_recv()
    vs[x] = (ub[x, c].astype(F32) + ur[x].astype(F32)).astype(BF16).reshape(NZ, 32, COLS)

    def gathered(dz):
        total = vs[x, (z + dz) % NZ].astype(F32)
        for k in (1, 3, 2):
            u_x(k, dz).wait_recv()
            total = total + vr[k, dz].astype(F32)
        return total

    for dz in (4, 5, 3, 6, 2, 7, 1):
        yo[dz] = gathered(dz).astype(BF16)
        u_z(dz).start()
    node = gathered(0)
    for k in (1, 7, 2, 6, 3, 5, 4):
        u_z(k).wait_recv()
        node = node + yr[k].astype(F32)
    high, low = split(node)
    partial = dot(high, w_hi[...], NT) + dot(high, w_lo[...], NT) + dot(low, w_hi[...], NT)
    for g in range(NY):
        po[g] = partial[g * 4:(g + 1) * 4].astype(BF16)
    loop(1, NY, lambda k: p_y(k).start())
    result = po[y].astype(F32)
    for k in range(1, NY):
        p_y(k).wait_recv()
        result = result + pr[k].astype(F32)
    grads_out[...] = result

    loop(1, NX, lambda k: a_x(k).wait_send())
    loop(1, NX, lambda k: b_x(k).wait_send())
    loop(1, NX, lambda k: r_x(k).wait_send())
    loop(1, NX, lambda k: t_x(k).wait_send())
    for k in range(1, NX):
        loop(0, NZ, lambda dz: u_x(k, dz).wait_send())
    loop(1, NZ, lambda k: b_z(k).wait_send())
    loop(1, NZ, lambda k: r_z(k).wait_send())
    loop(1, NZ, lambda k: t_z(k).wait_send())
    loop(1, NZ, lambda k: u_z(k).wait_send())
    loop(1, NY, lambda k: r_y(k).wait_send())
    loop(1, NY, lambda k: f_y(k).wait_send())
    loop(1, NY, lambda k: p_y(k).wait_send())
    loop(0, NX, lambda k: b_d(k).wait_send())
    loop(0, NX, lambda k: r_d(k).wait_send())
    loop(0, NX, lambda k: t_d(k).wait_send())
    loop(0, NX, lambda k: u_d(k).wait_send())
    for step in range(4):
        for way in range(2):
            for sub in range(2):
                if step < 3 or way == sub:
                    a_z(step, way, sub).wait_send()
    a_d(0, 0, 0).wait_send()
    a_d(0, 0, 1).wait_send()
    for step in range(1, 5):
        for way in range(2):
            for sub in range(2):
                if step < 4 or way == sub:
                    a_d(step, way, sub).wait_send()


def shards(texts, qkv_weight, norm_gain, routes, w_self, w_neigh, gnn_bias, neighbors, cotangent):
    vmem = pl.BlockSpec(memory_space=pltpu.VMEM)
    dma = pltpu.SemaphoreType.DMA
    hidden, grads = pl.pallas_call(
        kernel,
        out_shape=(
            jax.ShapeDtypeStruct((ROWS, 128), F32),
            jax.ShapeDtypeStruct((TITLES, D), F32),
        ),
        in_specs=[pl.BlockSpec(memory_space=pl.ANY)] * 9,
        out_specs=(vmem, vmem),
        scratch_shapes=[
            pltpu.VMEM((TITLES * SEQ, D), BF16),
            pltpu.VMEM((36, D), BF16),
            pltpu.VMEM((1, D), F32),
            pltpu.VMEM((TITLES, 8), jnp.int32),
            pltpu.VMEM((D, 128), F32),
            pltpu.VMEM((D, 128), F32),
            pltpu.VMEM((1, 128), F32),
            pltpu.VMEM((FAN, ROWS), jnp.int32),
            pltpu.VMEM((ROWS, 128), F32),
            dma((9,)),
            pltpu.VMEM((NC, NZ, NX, PIECE, 128), BF16),
            pltpu.VMEM((NC, NX, NZ, PIECE, 128), BF16),
            pltpu.VMEM((3 * D, D), BF16),
            pltpu.VMEM((3, TITLES, 256, SEQ), BF16),
            pltpu.VMEM((3, TITLES, SEQ, 256), BF16),
            pltpu.VMEM((3, TITLES, SEQ, 256), BF16),
            pltpu.VMEM((12, 8, 256), F32),
            pltpu.VMEM((ROWS, ROWS), BF16),
            pltpu.VMEM((ROWS, ROWS), BF16),
            pltpu.VMEM((D, COLS), BF16),
            pltpu.VMEM((D, COLS), BF16),
            pltpu.VMEM((NY, 8, 128), F32),
            pltpu.VMEM((NX, NC, NZ, 8, 128), F32),
            pltpu.VMEM((NX, 256, 512), BF16),
            pltpu.VMEM((NX, 512, 256), BF16),
            pltpu.VMEM((NY, TITLES, D), BF16),
            pltpu.VMEM((NX, NC, NZ, 32, COLS), BF16),
            pltpu.VMEM((ROWS, COLS), BF16),
            pltpu.VMEM((ROWS, COLS), BF16),
            pltpu.VMEM((NX, NC, 256, COLS), BF16),
            pltpu.VMEM((NX, 256, COLS), BF16),
            pltpu.VMEM((NX, NZ, 32, COLS), BF16),
            pltpu.VMEM((NX, NZ, 32, COLS), BF16),
            pltpu.VMEM((NZ, 32, COLS), BF16),
            pltpu.VMEM((NZ, 32, COLS), BF16),
            pltpu.VMEM((NY, TITLES, D), BF16),
            pltpu.VMEM((NY, TITLES, D), BF16),
            dma((NX,)), dma((NX,)),
            dma((4, 2, 2)), dma((4, 2, 2)),
            dma((5, 2, 2)), dma((5, 2, 2)),
            dma((NZ,)), dma((NZ,)),
            dma((NX,)), dma((NX,)),
            dma((NX,)), dma((NX,)),
            dma((NY,)), dma((NY,)),
            dma((NZ,)), dma((NZ,)),
            dma((NX,)), dma((NX,)),
            dma((NX,)), dma((NX,)),
            dma((NY,)), dma((NY,)),
            dma((NZ,)), dma((NZ,)),
            dma((NX,)), dma((NX,)),
            dma((NX,)), dma((NX,)),
            dma((NX,)), dma((NX,)),
            dma((NX, NZ)), dma((NX, NZ)),
            dma((NZ,)), dma((NZ,)),
            dma((NY,)), dma((NY,)),
        ],
        compiler_params=pltpu.CompilerParams(
            collective_id=0, has_side_effects=True, vmem_limit_bytes=60 * 2**20
        ),
        name="glem_step",
    )(
        texts.reshape(TITLES * SEQ, D),
        qkv_weight.T,
        norm_gain.reshape(1, D),
        routes,
        w_self,
        w_neigh,
        gnn_bias.reshape(1, 128),
        neighbors.T,
        cotangent,
    )
    return hidden, grads


def solution(mesh):
    placed = (
        P(("dp", "graph"), None, None),
        P(None, "dp"),
        P(),
        P(("dp", "graph"), None),
        P(None, "graph"),
        P(None, "graph"),
        P("graph"),
        P("dp", None),
        P("dp", "graph"),
    )
    return jax.shard_map(
        shards,
        mesh=mesh,
        in_specs=placed,
        out_specs=(P("dp", "graph"), P(("dp", "graph"), None)),
        check_vma=False,
    )
```

```python
import functools

import jax
import jax.numpy as jnp
from jax import lax
from jax.experimental import pallas as pl
from jax.experimental.pallas import tpu as pltpu
from jax.sharding import PartitionSpec as P

NX, NZ, NC, NY = 4, 8, 2, 8
D = 768
WIDE = 36
PIECE_A = 80
PIECE_B = 144
TITLES = 4
SEQ = 128
COLS = 256
ROWS = 1024
FAN = 15
BF16 = jnp.bfloat16
F32 = jnp.float32
NT = (((1,), (1,)), ((), ()))
NN = (((1,), (0,)), ((), ()))


def dot(a, b, dims=NN):
    return lax.dot_general(a, b, dims, preferred_element_type=F32)


def split(value):
    high = value.astype(BF16)
    return high, (value - high.astype(F32)).astype(BF16)


def iota(shape, axis):
    return lax.broadcasted_iota(jnp.int32, shape, axis)


def kernel(
    texts_in, wt_in, gain_in, routes_in, w_self_in, w_neigh_in, bias_in, near_in, cot_in,
    hidden_out, grads_out,
    texts, wt, gain, routes, w_self, w_neigh, bias, near, cot, load,
    wa, wb, dense, qt, keys, vals, pooled, adj_t, adj, w_hi, w_lo,
    ry, rt, sel, sel_t, feats, tg, xs, ds, ub, ur, vs, vr, yo, yr, po, pr,
    sa_x, ra_x, sa_z, ra_z, sa_d, ra_d, sb_z, rb_z, sb_x, rb_x, sb_d, rb_d,
    sr_y, rr_y, sr_z, rr_z, sr_x, rr_x, sr_d, rr_d,
    sf, rf, st_z, rt_z, st_x, rt_x, st_d, rt_d,
    su_d, ru_d, su_x, ru_x, su_z, ru_z, sp, rp,
):
    dp = lax.axis_index("dp")
    y = lax.axis_index("graph")
    x = dp // 16
    z = (dp // 2) % 8
    c = dp % 2
    other = 1 - c

    def at(px, pz, pc, py):
        return (px * 16 + pz * 2 + pc, py)

    def xp(k):
        return at((x + k) % NX, z, c, y)

    def zp(k):
        return at(x, (z + k) % NZ, c, y)

    def yp(k):
        return at(x, z, c, (y + k) % NY)

    mate = at(x, z, other, y)

    def send(src, dst, ssem, rsem, peer):
        return pltpu.make_async_remote_copy(
            src_ref=src, dst_ref=dst, send_sem=ssem, recv_sem=rsem,
            device_id=peer, device_id_type=pl.DeviceIdType.MESH,
        )

    def loop(low, high, body):
        def step(i, carry):
            body(i)
            return carry
        lax.fori_loop(low, high, step, 0)

    barrier = pltpu.get_barrier_semaphore()

    def greet(peer):
        pl.semaphore_signal(barrier, inc=1, device_id=peer, device_id_type=pl.DeviceIdType.MESH)

    for k in (4, 3, 5, 2, 6, 1, 7):
        greet(zp(k))
        greet(yp(k))
    for k in (2, 1, 3):
        greet(xp(k))
    greet(mate)

    held = (texts, wt, gain, routes, w_self, w_neigh, bias, near, cot)
    given = (texts_in, wt_in, gain_in, routes_in, w_self_in, w_neigh_in, bias_in, near_in, cot_in)
    loads = [pltpu.make_async_copy(given[i], held[i], load.at[i]) for i in range(9)]
    for i in (1, 3, 7, 4, 5, 0, 2, 6, 8):
        loads[i].start()

    def a_x(k):
        return send(wa.at[c, z, x], wa.at[c, z, x], sa_x.at[k], ra_x.at[k], xp(k))

    def ring(step, way, sub):
        hops = step if way == 0 else -step
        return wa.at[c, (z - hops + NZ) % NZ, pl.ds(2 * sub, 2)]

    def a_z(step, way, sub):
        part = ring(step, way, sub)
        peer = zp(1) if way == 0 else zp(NZ - 1)
        return send(part, part, sa_z.at[step, way, sub], ra_z.at[step, way, sub], peer)

    def a_d(step, way):
        if step == 4:
            part = ring(step, way, way)
        else:
            part = wa.at[c, (z - (step if way == 0 else -step) + NZ) % NZ]
        return send(part, part, sa_d.at[step, way], ra_d.at[step, way], mate)

    def b_z(k):
        return send(wb.at[c, x, z], wb.at[c, x, z], sb_z.at[k], rb_z.at[k], zp(k))

    def b_x(k):
        return send(wb.at[c, x], wb.at[c, x], sb_x.at[k], rb_x.at[k], xp(k))

    def b_s(k, dz):
        part = wb.at[c, x, (z + dz) % NZ]
        return send(part, part, sb_x.at[k], rb_x.at[k], xp(k))

    def b_d(k):
        part = wb.at[c, (x - k + NX) % NX]
        return send(part, part, sb_d.at[k], rb_d.at[k], mate)

    def r_y(k):
        return send(ry.at[y], ry.at[y], sr_y.at[k], rr_y.at[k], yp(k))

    def r_z(k):
        return send(rt.at[x, c, z], rt.at[x, c, z], sr_z.at[k], rr_z.at[k], zp(k))

    def r_x(k):
        return send(rt.at[x, c], rt.at[x, c], sr_x.at[k], rr_x.at[k], xp(k))

    def r_d(k):
        part = rt.at[(x - k + NX) % NX, c]
        return send(part, part, sr_d.at[k], rr_d.at[k], mate)

    def f_y(k):
        return send(feats.at[y], feats.at[y], sf.at[k], rf.at[k], yp(k))

    def t_z(k):
        return send(tg.at[x, c, z], tg.at[x, c, z], st_z.at[k], rt_z.at[k], zp(k))

    def t_x(k):
        return send(tg.at[x, c], tg.at[x, c], st_x.at[k], rt_x.at[k], xp(k))

    def t_s(k, dz):
        part = tg.at[x, c, (z + dz) % NZ]
        return send(part, part, st_x.at[k], rt_x.at[k], xp(k))

    def t_d(k):
        part = tg.at[(x - k + NX) % NX, c]
        return send(part, part, st_d.at[k], rt_d.at[k], mate)

    def u_d(k):
        to = (x + k) % NX
        return send(ub.at[to, other], ur.at[to], su_d.at[k], ru_d.at[k], mate)

    def u_x(k, dz):
        to = (z + dz) % NZ
        return send(vs.at[(x + k) % NX, to], vr.at[k, dz], su_x.at[k, dz], ru_x.at[k, dz], xp(k))

    def u_z(k):
        return send(yo.at[k], yr.at[k], su_z.at[k], ru_z.at[k], zp(k))

    def p_y(k):
        return send(po.at[(y + k) % NY], pr.at[k], sp.at[k], rp.at[k], yp(k))

    loads[1].wait()
    shard = wt[...].astype(F32)
    filling = jnp.zeros((PIECE_A - 2 * WIDE, 128), F32)
    tiles = [shard[:, i * 128:(i + 1) * 128] for i in range(6)]
    wa[c, z, x] = jnp.concatenate(tiles[:2] + [filling], axis=0).astype(BF16)
    wb[c, x, z] = jnp.concatenate(tiles[2:], axis=0).astype(BF16)
    loads[3].wait()
    row = iota((8, 128), 0)
    spread = ((iota((8, 128), 1) % 8) == iota((8, 128), 0)).astype(BF16)
    tiled = dot(routes[...].astype(F32).astype(BF16), spread)
    own = jnp.sum(jnp.where((iota((TITLES, 128), 1) // 8) == iota((TITLES, 128), 0), tiled, 0.0), axis=0, keepdims=True)
    ry[y] = jnp.where(row == y, jnp.broadcast_to(own, (8, 128)), 0.0)

    pl.semaphore_wait(barrier, 1 + (NX - 1) + (NZ - 1) + (NY - 1))

    loop(1, NX, lambda k: a_x(k).start())
    for k in (1, 7, 2, 6, 3, 5, 4):
        b_z(k).start()
    for k in range(1, NX):
        b_s(k, 0).start()
    loop(1, NY, lambda k: r_y(k).start())

    def count(first, last):
        def body(step):
            j0 = pl.multiple_of((step // 4) * 64, 64)
            i0 = pl.multiple_of((step % 4) * 256, 256)
            rows = iota((64, 256), 0) + j0
            total = jnp.zeros((64, 256), F32)
            for k in range(FAN):
                total = total + jnp.where(rows == near[k:k + 1, pl.ds(i0, 256)], 1.0, 0.0)
            adj_t[pl.ds(j0, 64), pl.ds(i0, 256)] = total.astype(BF16)
        loop(first, last, body)

    def flip(step):
        r0 = pl.multiple_of((step // 4) * 256, 256)
        c0 = pl.multiple_of((step % 4) * 256, 256)
        adj[pl.ds(r0, 256), pl.ds(c0, 256)] = adj_t[pl.ds(c0, 256), pl.ds(r0, 256)].astype(F32).T.astype(BF16)

    def pass_b(k):
        b_z(k).wait_recv()
        for n in range(1, NX):
            b_s(n, NZ - k).start()

    def pass_a(step):
        for sub in range(2):
            for way in range(2):
                a_z(step, way, sub).wait_recv()
                if step < 2 or way == sub:
                    a_z(step + 1, way, sub).start()
        for way in range(2):
            a_d(step + 1, way).start()

    loads[7].wait()
    count(0, 24)
    loop(1, NX, lambda k: a_x(k).wait_recv())
    for sub in range(2):
        for way in range(2):
            a_z(0, way, sub).start()
    a_d(0, 0).start()
    pass_b(1)
    pass_b(7)
    count(24, 32)
    pass_b(2)
    pass_b(6)
    pass_a(0)
    pass_b(3)
    pass_b(5)
    pass_b(4)
    b_d(0).start()
    count(32, 38)
    pass_a(1)
    loop(1, NY, lambda k: r_y(k).wait_recv())
    rt[x, c, z] = jnp.sum(ry[...], axis=0)
    loop(1, NZ, lambda k: r_z(k).start())
    pass_a(2)

    for k in (1, 3, 2):
        b_x(k).wait_recv()
        b_d(k).start()
    a_z(3, 0, 0).wait_recv()
    a_d(4, 0).start()
    a_z(3, 1, 1).wait_recv()
    a_d(4, 1).start()
    a_d(0, 0).wait_recv()
    for step in range(1, 4):
        for way in range(2):
            a_d(step, way).wait_recv()
    loop(0, NX, lambda k: b_d(k).wait_recv())
    a_d(4, 0).wait_recv()
    a_d(4, 1).wait_recv()
    loads[0].wait()
    loads[2].wait()
    loads[6].wait()
    loads[8].wait()

    loop(1, NZ, lambda k: r_z(k).wait_recv())
    loop(1, NX, lambda k: r_x(k).start())
    r_d(0).start()

    def pack(group):
        gx = group // 4
        gz = (group % 4) * 2
        base = pl.multiple_of(group * 144, 16)
        left = [wa[cc, gz + dz, gx].astype(F32) for dz in range(2) for cc in range(2)]
        right = [wb[cc, gx, gz + dz].astype(F32) for dz in range(2) for cc in range(2)]
        for i in range(6):
            pieces = left if i < 2 else right
            first = (i if i < 2 else i - 2) * WIDE
            column = jnp.concatenate([piece[first:first + WIDE] for piece in pieces], axis=0)
            dense[pl.ds(base, 144), i * 128:(i + 1) * 128] = column.astype(BF16)

    loop(0, 16, pack)

    def project(block):
        at0 = pl.multiple_of(block * 256, 256)
        rows = pl.ds(at0, 256)
        title_q = dot(dense[rows, :], texts[...], NT).astype(BF16)
        for t in range(TITLES):
            qt[block, t] = title_q[:, t * SEQ:(t + 1) * SEQ]
        rows = pl.ds(pl.multiple_of(at0 + D, 256), 256)
        keys[block] = dot(texts[...], dense[rows, :], NT).astype(BF16).reshape(TITLES, SEQ, 256)
        rows = pl.ds(pl.multiple_of(at0 + 2 * D, 256), 256)
        vals[block] = dot(texts[...], dense[rows, :], NT).astype(BF16).reshape(TITLES, SEQ, 256)

    loop(0, 3, project)

    loop(1, NX, lambda k: r_x(k).wait_recv())
    loop(1, NX, lambda k: r_d(k).start())

    adder = jnp.where((iota((8, 4 * SEQ), 1) // SEQ) == (iota((8, 4 * SEQ), 0) % 4), 1.0, 0.0).astype(BF16)
    upper = iota((8, SEQ), 0) < 4
    own_head = (iota((8, 256), 1) // 64) == (iota((8, 256), 0) % 4)
    blank = jnp.zeros((64, SEQ), BF16)

    def attend(block):
        each = range(TITLES)
        scores = []
        for t in each:
            q = qt[block, t]
            queries = jnp.concatenate(
                [
                    jnp.concatenate([q[h * 64:(h + 1) * 64] if i == h else blank for i in range(4)], axis=1)
                    for h in range(4)
                ],
                axis=0,
            )
            scores.append(dot(keys[block, t], queries) * 0.125)
        scores = [jnp.exp(s - jnp.max(s, axis=0, keepdims=True)) for s in scores]
        probs = [(s * (1.0 / jnp.sum(s, axis=0, keepdims=True))).astype(BF16) for s in scores]
        sums = [split(dot(adder, p, NT)) for p in probs]
        sums = [jnp.where(upper, high.astype(F32), low.astype(F32)).astype(BF16) for high, low in sums]
        mixed = [dot(sums[t], vals[block, t]) for t in each]
        for t in each:
            row = jnp.sum(jnp.where(own_head, mixed[t], 0.0), axis=0, keepdims=True) * (1.0 / SEQ)
            pooled[block * TITLES + t] = jnp.broadcast_to(row, (8, 256))

    loop(0, 3, attend)

    means = jnp.concatenate(
        [
            jnp.concatenate([pooled[b * TITLES + t][0:1] for b in range(3)], axis=1)
            for t in range(TITLES)
        ],
        axis=0,
    )
    center = jnp.mean(means, axis=1, keepdims=True)
    variance = jnp.mean((means - center) ** 2, axis=1, keepdims=True)
    feats[y] = ((means - center) / jnp.sqrt(variance + 1e-05) * gain[...]).astype(BF16)

    for k in (4, 3, 5, 2, 6, 1, 7):
        f_y(k).start()
    loads[4].wait()
    loads[5].wait()
    w_hi[:, :128], w_lo[:, :128] = split(w_self[...])
    w_hi[:, 128:], w_lo[:, 128:] = split(w_neigh[...])
    count(38, 52)
    loop(0, NX, lambda k: r_d(k).wait_recv())
    title = iota((128, 512), 1)
    named = iota((128, 512), 0)
    same = jnp.where((named < 32) & (named // 8 == title % 4), 1.0, 0.0).astype(BF16)
    ahead = jnp.where((named < 32) & (named // 8 < title % 4), 1.0, 0.0).astype(BF16)
    mine = (title // 4) == named
    slot = iota((256, 512), 0)
    col = iota((256, 512), 1)
    match = (
        (slot // 32 == (col % 32) // 4)
        & ((slot % 32) // 4 == (col % 256) // 32)
        & ((slot % 4) // 2 == col // 256)
    )
    wanted = jnp.where(match, (slot % 2).astype(F32) + 1.0, -1.0)

    def select(block):
        listed = rt[block].reshape(128, 128)
        hits = jnp.where(listed == dp.astype(F32), 1.0, 0.0).astype(BF16)
        code = dot(hits, same) * (1.0 + dot(hits, ahead))
        code = jnp.sum(jnp.where(mine, code, 0.0), axis=0, keepdims=True)
        chosen = jnp.where(code == wanted, 1.0, 0.0)
        sel[block] = chosen.astype(BF16)
        sel_t[block] = chosen.T.astype(BF16)

    loop(0, NX, select)

    loop(1, NY, lambda k: f_y(k).wait_recv())
    group_feats = jnp.concatenate([feats[g].astype(F32) for g in range(NY)], axis=0).astype(BF16)
    tg[x, c, z] = (dot(group_feats, w_hi[...]) + dot(group_feats, w_lo[...])).astype(BF16)

    for k in (4, 3, 5):
        t_z(k).start()
    for k in range(1, NX):
        t_s(k, 0).start()
    for k in (2, 6, 1, 7):
        t_z(k).start()
    count(52, 64)
    loop(0, 16, flip)
    for k in (1, 7, 2, 6, 3, 5, 4):
        t_z(k).wait_recv()
        for n in range(1, NX):
            t_s(n, NZ - k).start()
    t_d(0).start()

    def place(block):
        rows = dot(sel[block], tg[block].reshape(512, COLS)).astype(BF16)
        for g in range(NY):
            xs[pl.ds(pl.multiple_of(g * 128 + block * 32, 32), 32), :] = rows[g * 32:(g + 1) * 32]

    t_d(0).wait_recv()
    place(x)
    for k in (1, 3, 2):
        t_x(k).wait_recv()
        t_d(k).start()
    for k in (1, 3, 2):
        t_d(k).wait_recv()
        place((x - k + NX) % NX)

    def layer(step):
        rows = pl.ds(step * 256, 256)
        total = xs[rows, :128].astype(F32) + dot(adj[rows, :], xs[:, 128:]) + bias[...]
        gate = 1.0 / (1.0 + jnp.exp(-total))
        hidden_out[rows, :] = total * gate
        ds[rows, :128] = (cot[rows, :] * gate * (1.0 + total * (1.0 - gate))).astype(BF16)

    for step in range(4):
        layer(step)

    def backward(step):
        rows = pl.ds(step * 256, 256)
        ds[rows, 128:] = dot(adj_t[rows, :], ds[:, :128]).astype(BF16)

    for step in range(4):
        backward(step)

    def titles_of(block):
        rows = jnp.concatenate(
            [ds[pl.ds(pl.multiple_of(g * 128 + block * 32, 32), 32), :] for g in range(NY)], axis=0
        )
        ub[block] = dot(sel_t[block], rows).astype(BF16).reshape(NC, 256, COLS)

    for k in (1, 2, 3, 0):
        titles_of((x + k) % NX)
        u_d(k).start()
    for k in (1, 2, 3):
        to = (x + k) % NX
        u_d(k).wait_recv()
        vs[to] = (ub[to, c].astype(F32) + ur[to].astype(F32)).astype(BF16).reshape(NZ, 32, COLS)
        for dz in (4, 5, 3, 6, 2, 7, 1, 0):
            u_x(k, dz).start()
    u_d(0).wait_recv()
    vs[x] = (ub[x, c].astype(F32) + ur[x].astype(F32)).astype(BF16).reshape(NZ, 32, COLS)

    def gathered(dz):
        total = vs[x, (z + dz) % NZ].astype(F32)
        for k in (1, 3, 2):
            u_x(k, dz).wait_recv()
            total = total + vr[k, dz].astype(F32)
        return total

    for dz in (4, 5, 3, 6, 2, 7, 1):
        yo[dz] = gathered(dz).astype(BF16)
        u_z(dz).start()
    node = gathered(0)
    for k in (1, 7, 2, 6, 3, 5, 4):
        u_z(k).wait_recv()
        node = node + yr[k].astype(F32)
    high, low = split(node)
    partial = dot(high, w_hi[...], NT) + dot(high, w_lo[...], NT) + dot(low, w_hi[...], NT)
    for g in range(NY):
        po[g] = partial[g * 4:(g + 1) * 4].astype(BF16)
    for k in (4, 3, 5, 2, 6, 1, 7):
        p_y(k).start()
    result = po[y].astype(F32)
    for k in range(1, NY):
        p_y(k).wait_recv()
        result = result + pr[k].astype(F32)
    grads_out[...] = result

    loop(1, NX, lambda k: a_x(k).wait_send())
    loop(1, NX, lambda k: b_x(k).wait_send())
    loop(1, NX, lambda k: r_x(k).wait_send())
    loop(1, NX, lambda k: t_x(k).wait_send())
    for k in range(1, NX):
        loop(0, NZ, lambda dz: u_x(k, dz).wait_send())
    loop(1, NZ, lambda k: b_z(k).wait_send())
    loop(1, NZ, lambda k: r_z(k).wait_send())
    loop(1, NZ, lambda k: t_z(k).wait_send())
    loop(1, NZ, lambda k: u_z(k).wait_send())
    loop(1, NY, lambda k: r_y(k).wait_send())
    loop(1, NY, lambda k: f_y(k).wait_send())
    loop(1, NY, lambda k: p_y(k).wait_send())
    loop(0, NX, lambda k: b_d(k).wait_send())
    loop(0, NX, lambda k: r_d(k).wait_send())
    loop(0, NX, lambda k: t_d(k).wait_send())
    loop(0, NX, lambda k: u_d(k).wait_send())
    for step in range(4):
        for way in range(2):
            for sub in range(2):
                if step < 3 or way == sub:
                    a_z(step, way, sub).wait_send()
    a_d(0, 0).wait_send()
    for step in range(1, 5):
        for way in range(2):
            a_d(step, way).wait_send()


def shards(texts, qkv_weight, norm_gain, routes, w_self, w_neigh, gnn_bias, neighbors, cotangent):
    vmem = pl.BlockSpec(memory_space=pltpu.VMEM)
    dma = pltpu.SemaphoreType.DMA
    hidden, grads = pl.pallas_call(
        kernel,
        out_shape=(
            jax.ShapeDtypeStruct((ROWS, 128), F32),
            jax.ShapeDtypeStruct((TITLES, D), F32),
        ),
        in_specs=[pl.BlockSpec(memory_space=pl.ANY)] * 9,
        out_specs=(vmem, vmem),
        scratch_shapes=[
            pltpu.VMEM((TITLES * SEQ, D), BF16),
            pltpu.VMEM((36, D), BF16),
            pltpu.VMEM((1, D), F32),
            pltpu.VMEM((TITLES, 8), jnp.int32),
            pltpu.VMEM((D, 128), F32),
            pltpu.VMEM((D, 128), F32),
            pltpu.VMEM((1, 128), F32),
            pltpu.VMEM((FAN, ROWS), jnp.int32),
            pltpu.VMEM((ROWS, 128), F32),
            dma((9,)),
            pltpu.VMEM((NC, NZ, NX, PIECE_A, 128), BF16),
            pltpu.VMEM((NC, NX, NZ, PIECE_B, 128), BF16),
            pltpu.VMEM((3 * D, D), BF16),
            pltpu.VMEM((3, TITLES, 256, SEQ), BF16),
            pltpu.VMEM((3, TITLES, SEQ, 256), BF16),
            pltpu.VMEM((3, TITLES, SEQ, 256), BF16),
            pltpu.VMEM((12, 8, 256), F32),
            pltpu.VMEM((ROWS, ROWS), BF16),
            pltpu.VMEM((ROWS, ROWS), BF16),
            pltpu.VMEM((D, COLS), BF16),
            pltpu.VMEM((D, COLS), BF16),
            pltpu.VMEM((NY, 8, 128), F32),
            pltpu.VMEM((NX, NC, NZ, 8, 128), F32),
            pltpu.VMEM((NX, 256, 512), BF16),
            pltpu.VMEM((NX, 512, 256), BF16),
            pltpu.VMEM((NY, TITLES, D), BF16),
            pltpu.VMEM((NX, NC, NZ, 32, COLS), BF16),
            pltpu.VMEM((ROWS, COLS), BF16),
            pltpu.VMEM((ROWS, COLS), BF16),
            pltpu.VMEM((NX, NC, 256, COLS), BF16),
            pltpu.VMEM((NX, 256, COLS), BF16),
            pltpu.VMEM((NX, NZ, 32, COLS), BF16),
            pltpu.VMEM((NX, NZ, 32, COLS), BF16),
            pltpu.VMEM((NZ, 32, COLS), BF16),
            pltpu.VMEM((NZ, 32, COLS), BF16),
            pltpu.VMEM((NY, TITLES, D), BF16),
            pltpu.VMEM((NY, TITLES, D), BF16),
            dma((NX,)), dma((NX,)),
            dma((4, 2, 2)), dma((4, 2, 2)),
            dma((5, 2)), dma((5, 2)),
            dma((NZ,)), dma((NZ,)),
            dma((NX,)), dma((NX,)),
            dma((NX,)), dma((NX,)),
            dma((NY,)), dma((NY,)),
            dma((NZ,)), dma((NZ,)),
            dma((NX,)), dma((NX,)),
            dma((NX,)), dma((NX,)),
            dma((NY,)), dma((NY,)),
            dma((NZ,)), dma((NZ,)),
            dma((NX,)), dma((NX,)),
            dma((NX,)), dma((NX,)),
            dma((NX,)), dma((NX,)),
            dma((NX, NZ)), dma((NX, NZ)),
            dma((NZ,)), dma((NZ,)),
            dma((NY,)), dma((NY,)),
        ],
        compiler_params=pltpu.CompilerParams(
            collective_id=0, has_side_effects=True, vmem_limit_bytes=60 * 2**20
        ),
        name="glem_step",
    )(
        texts.reshape(TITLES * SEQ, D),
        qkv_weight.T,
        norm_gain.reshape(1, D),
        routes,
        w_self,
        w_neigh,
        gnn_bias.reshape(1, 128),
        neighbors.T,
        cotangent,
    )
    return hidden, grads


def solution(mesh):
    placed = (
        P(("dp", "graph"), None, None),
        P(None, "dp"),
        P(),
        P(("dp", "graph"), None),
        P(None, "graph"),
        P(None, "graph"),
        P("graph"),
        P("dp", None),
        P("dp", "graph"),
    )
    return jax.shard_map(
        shards,
        mesh=mesh,
        in_specs=placed,
        out_specs=(P("dp", "graph"), P(("dp", "graph"), None)),
        check_vma=False,
    )
```

```python
import functools

import jax
import jax.numpy as jnp
from jax import lax
from jax.experimental import pallas as pl
from jax.experimental.pallas import tpu as pltpu
from jax.sharding import PartitionSpec as P

NX, NZ, NC, NY = 4, 8, 2, 8
D = 768
WIDE = 36
PIECE_A = 80
PIECE_B = 144
TITLES = 4
SEQ = 128
COLS = 256
ROWS = 1024
FAN = 15
BF16 = jnp.bfloat16
F32 = jnp.float32
NT = (((1,), (1,)), ((), ()))
NN = (((1,), (0,)), ((), ()))


def dot(a, b, dims=NN):
    return lax.dot_general(a, b, dims, preferred_element_type=F32)


def split(value):
    high = value.astype(BF16)
    return high, (value - high.astype(F32)).astype(BF16)


def iota(shape, axis):
    return lax.broadcasted_iota(jnp.int32, shape, axis)


def kernel(
    texts_in, wt_in, gain_in, routes_in, w_self_in, w_neigh_in, bias_in, near_in, cot_in,
    hidden_out, grads_out,
    texts, wt, gain, routes, w_self, w_neigh, bias, near, cot, load,
    wa, wb, dense, qt, keys, vals, pooled, adj_t, adj, w_hi, w_lo,
    ry, rt, sel, sel_t, feats, tg, xs, ds, ub, ur, vs, vr, yo, yr, po, pr,
    sa_x, ra_x, sa_z, ra_z, sa_d, ra_d, sb_z, rb_z, sb_x, rb_x, sb_d, rb_d,
    sr_y, rr_y, sr_z, rr_z, sr_x, rr_x, sr_d, rr_d,
    sf, rf, st_z, rt_z, st_x, rt_x, st_d, rt_d,
    su_d, ru_d, su_x, ru_x, su_z, ru_z, sp, rp,
):
    dp = lax.axis_index("dp")
    y = lax.axis_index("graph")
    x = dp // 16
    z = (dp // 2) % 8
    c = dp % 2
    other = 1 - c

    def at(px, pz, pc, py):
        return (px * 16 + pz * 2 + pc, py)

    def xp(k):
        return at((x + k) % NX, z, c, y)

    def zp(k):
        return at(x, (z + k) % NZ, c, y)

    def yp(k):
        return at(x, z, c, (y + k) % NY)

    mate = at(x, z, other, y)

    def send(src, dst, ssem, rsem, peer):
        return pltpu.make_async_remote_copy(
            src_ref=src, dst_ref=dst, send_sem=ssem, recv_sem=rsem,
            device_id=peer, device_id_type=pl.DeviceIdType.MESH,
        )

    def loop(low, high, body):
        def step(i, carry):
            body(i)
            return carry
        lax.fori_loop(low, high, step, 0)

    barrier = pltpu.get_barrier_semaphore()

    def greet(peer):
        pl.semaphore_signal(barrier, inc=1, device_id=peer, device_id_type=pl.DeviceIdType.MESH)

    for k in (4, 3, 5, 2, 6, 1, 7):
        greet(zp(k))
        greet(yp(k))
    for k in (2, 1, 3):
        greet(xp(k))
    greet(mate)

    held = (texts, wt, gain, routes, w_self, w_neigh, bias, near, cot)
    given = (texts_in, wt_in, gain_in, routes_in, w_self_in, w_neigh_in, bias_in, near_in, cot_in)
    loads = [pltpu.make_async_copy(given[i], held[i], load.at[i]) for i in range(9)]
    for i in (1, 3, 7, 4, 5, 0, 2, 6, 8):
        loads[i].start()

    def a_x(k):
        return send(wa.at[c, z, x], wa.at[c, z, x], sa_x.at[k], ra_x.at[k], xp(k))

    def ring(step, way, sub):
        hops = step if way == 0 else -step
        return wa.at[c, (z - hops + NZ) % NZ, pl.ds(2 * sub, 2)]

    def a_z(step, way, sub):
        part = ring(step, way, sub)
        peer = zp(1) if way == 0 else zp(NZ - 1)
        return send(part, part, sa_z.at[step, way, sub], ra_z.at[step, way, sub], peer)

    def a_d(step, way):
        if step == 4:
            part = ring(step, way, way)
        else:
            part = wa.at[c, (z - (step if way == 0 else -step) + NZ) % NZ]
        return send(part, part, sa_d.at[step, way], ra_d.at[step, way], mate)

    def b_z(k):
        return send(wb.at[c, x, z], wb.at[c, x, z], sb_z.at[k], rb_z.at[k], zp(k))

    def b_x(k):
        return send(wb.at[c, x], wb.at[c, x], sb_x.at[k], rb_x.at[k], xp(k))

    def b_s(k, dz):
        part = wb.at[c, x, (z + dz) % NZ]
        return send(part, part, sb_x.at[k], rb_x.at[k], xp(k))

    def b_d(k):
        part = wb.at[c, (x - k + NX) % NX]
        return send(part, part, sb_d.at[k], rb_d.at[k], mate)

    def r_y(k):
        return send(ry.at[y], ry.at[y], sr_y.at[k], rr_y.at[k], yp(k))

    def r_z(k):
        return send(rt.at[x, c, z], rt.at[x, c, z], sr_z.at[k], rr_z.at[k], zp(k))

    def r_x(k):
        return send(rt.at[x, c], rt.at[x, c], sr_x.at[k], rr_x.at[k], xp(k))

    def r_d(k):
        part = rt.at[(x - k + NX) % NX, c]
        return send(part, part, sr_d.at[k], rr_d.at[k], mate)

    def f_y(k):
        return send(feats.at[y], feats.at[y], sf.at[k], rf.at[k], yp(k))

    def t_z(k):
        return send(tg.at[x, c, z], tg.at[x, c, z], st_z.at[k], rt_z.at[k], zp(k))

    def t_x(k):
        return send(tg.at[x, c], tg.at[x, c], st_x.at[k], rt_x.at[k], xp(k))

    def t_s(k, dz):
        part = tg.at[x, c, (z + dz) % NZ]
        return send(part, part, st_x.at[k], rt_x.at[k], xp(k))

    def t_d(k):
        part = tg.at[(x - k + NX) % NX, c]
        return send(part, part, st_d.at[k], rt_d.at[k], mate)

    def u_d(k):
        to = (x + k) % NX
        return send(ub.at[to, other], ur.at[to], su_d.at[k], ru_d.at[k], mate)

    def u_x(k, dz):
        to = (z + dz) % NZ
        return send(vs.at[(x + k) % NX, to], vr.at[k, dz], su_x.at[k, dz], ru_x.at[k, dz], xp(k))

    def u_z(k):
        return send(yo.at[k], yr.at[k], su_z.at[k], ru_z.at[k], zp(k))

    def p_y(k):
        return send(po.at[(y + k) % NY], pr.at[k], sp.at[k], rp.at[k], yp(k))

    loads[1].wait()
    shard = wt[...].astype(F32)
    filling = jnp.zeros((PIECE_A - 2 * WIDE, 128), F32)
    tiles = [shard[:, i * 128:(i + 1) * 128] for i in range(6)]
    wa[c, z, x] = jnp.concatenate(tiles[:2] + [filling], axis=0).astype(BF16)
    wb[c, x, z] = jnp.concatenate(tiles[2:], axis=0).astype(BF16)
    loads[3].wait()
    row = iota((8, 128), 0)
    spread = ((iota((8, 128), 1) % 8) == iota((8, 128), 0)).astype(BF16)
    tiled = dot(routes[...].astype(F32).astype(BF16), spread)
    own = jnp.sum(jnp.where((iota((TITLES, 128), 1) // 8) == iota((TITLES, 128), 0), tiled, 0.0), axis=0, keepdims=True)
    ry[y] = jnp.where(row == y, jnp.broadcast_to(own, (8, 128)), 0.0)

    pl.semaphore_wait(barrier, 1 + (NX - 1) + (NZ - 1) + (NY - 1))

    loop(1, NX, lambda k: a_x(k).start())
    for k in (1, 7, 2, 6, 3, 5, 4):
        b_z(k).start()
    for k in range(1, NX):
        b_s(k, 0).start()
    loop(1, NY, lambda k: r_y(k).start())

    def count(first, last):
        def body(step):
            j0 = pl.multiple_of((step // 4) * 64, 64)
            i0 = pl.multiple_of((step % 4) * 256, 256)
            rows = iota((64, 256), 0) + j0
            total = jnp.zeros((64, 256), F32)
            for k in range(FAN):
                total = total + jnp.where(rows == near[k:k + 1, pl.ds(i0, 256)], 1.0, 0.0)
            adj_t[pl.ds(j0, 64), pl.ds(i0, 256)] = total.astype(BF16)
        loop(first, last, body)

    def flip(step):
        r0 = pl.multiple_of((step // 4) * 256, 256)
        c0 = pl.multiple_of((step % 4) * 256, 256)
        adj[pl.ds(r0, 256), pl.ds(c0, 256)] = adj_t[pl.ds(c0, 256), pl.ds(r0, 256)].astype(F32).T.astype(BF16)

    def pass_b(k):
        b_z(k).wait_recv()
        for n in range(1, NX):
            b_s(n, NZ - k).start()

    def pass_a(step):
        for sub in range(2):
            for way in range(2):
                a_z(step, way, sub).wait_recv()
                if step < 2 or way == sub:
                    a_z(step + 1, way, sub).start()
        for way in range(2):
            a_d(step + 1, way).start()

    loads[7].wait()
    count(0, 24)
    loop(1, NX, lambda k: a_x(k).wait_recv())
    for sub in range(2):
        for way in range(2):
            a_z(0, way, sub).start()
    a_d(0, 0).start()
    pass_b(1)
    pass_b(7)
    count(24, 32)
    pass_b(2)
    pass_b(6)
    pass_a(0)
    pass_b(3)
    pass_b(5)
    pass_a(1)
    pass_b(4)
    b_d(0).start()
    count(32, 38)
    loop(1, NY, lambda k: r_y(k).wait_recv())
    rt[x, c, z] = jnp.sum(ry[...], axis=0)
    loop(1, NZ, lambda k: r_z(k).start())
    pass_a(2)

    for k in (1, 3, 2):
        b_x(k).wait_recv()
        b_d(k).start()
    a_z(3, 0, 0).wait_recv()
    a_d(4, 0).start()
    a_z(3, 1, 1).wait_recv()
    a_d(4, 1).start()
    a_d(0, 0).wait_recv()
    for step in range(1, 4):
        for way in range(2):
            a_d(step, way).wait_recv()
    loop(0, NX, lambda k: b_d(k).wait_recv())
    a_d(4, 0).wait_recv()
    a_d(4, 1).wait_recv()
    loads[0].wait()
    loads[2].wait()
    loads[6].wait()
    loads[8].wait()

    loop(1, NZ, lambda k: r_z(k).wait_recv())
    loop(1, NX, lambda k: r_x(k).start())
    r_d(0).start()

    def pack(group):
        gx = group // 4
        gz = (group % 4) * 2
        base = pl.multiple_of(group * 144, 16)
        left = [wa[cc, gz + dz, gx].astype(F32) for dz in range(2) for cc in range(2)]
        right = [wb[cc, gx, gz + dz].astype(F32) for dz in range(2) for cc in range(2)]
        for i in range(6):
            pieces = left if i < 2 else right
            first = (i if i < 2 else i - 2) * WIDE
            column = jnp.concatenate([piece[first:first + WIDE] for piece in pieces], axis=0)
            dense[pl.ds(base, 144), i * 128:(i + 1) * 128] = column.astype(BF16)

    loop(0, 16, pack)

    def project(block):
        at0 = pl.multiple_of(block * 256, 256)
        rows = pl.ds(at0, 256)
        title_q = dot(dense[rows, :], texts[...], NT).astype(BF16)
        for t in range(TITLES):
            qt[block, t] = title_q[:, t * SEQ:(t + 1) * SEQ]
        rows = pl.ds(pl.multiple_of(at0 + D, 256), 256)
        keys[block] = dot(texts[...], dense[rows, :], NT).astype(BF16).reshape(TITLES, SEQ, 256)
        rows = pl.ds(pl.multiple_of(at0 + 2 * D, 256), 256)
        vals[block] = dot(texts[...], dense[rows, :], NT).astype(BF16).reshape(TITLES, SEQ, 256)

    loop(0, 3, project)

    loop(1, NX, lambda k: r_x(k).wait_recv())
    loop(1, NX, lambda k: r_d(k).start())

    adder = jnp.where((iota((8, 4 * SEQ), 1) // SEQ) == (iota((8, 4 * SEQ), 0) % 4), 1.0, 0.0).astype(BF16)
    upper = iota((8, SEQ), 0) < 4
    own_head = (iota((8, 256), 1) // 64) == (iota((8, 256), 0) % 4)
    blank = jnp.zeros((64, SEQ), BF16)

    def attend(block):
        each = range(TITLES)
        scores = []
        for t in each:
            q = qt[block, t]
            queries = jnp.concatenate(
                [
                    jnp.concatenate([q[h * 64:(h + 1) * 64] if i == h else blank for i in range(4)], axis=1)
                    for h in range(4)
                ],
                axis=0,
            )
            scores.append(dot(keys[block, t], queries) * 0.125)
        scores = [jnp.exp(s - jnp.max(s, axis=0, keepdims=True)) for s in scores]
        probs = [(s * (1.0 / jnp.sum(s, axis=0, keepdims=True))).astype(BF16) for s in scores]
        sums = [split(dot(adder, p, NT)) for p in probs]
        sums = [jnp.where(upper, high.astype(F32), low.astype(F32)).astype(BF16) for high, low in sums]
        mixed = [dot(sums[t], vals[block, t]) for t in each]
        for t in each:
            row = jnp.sum(jnp.where(own_head, mixed[t], 0.0), axis=0, keepdims=True) * (1.0 / SEQ)
            pooled[block * TITLES + t] = jnp.broadcast_to(row, (8, 256))

    loop(0, 3, attend)

    means = jnp.concatenate(
        [
            jnp.concatenate([pooled[b * TITLES + t][0:1] for b in range(3)], axis=1)
            for t in range(TITLES)
        ],
        axis=0,
    )
    center = jnp.mean(means, axis=1, keepdims=True)
    variance = jnp.mean((means - center) ** 2, axis=1, keepdims=True)
    feats[y] = ((means - center) / jnp.sqrt(variance + 1e-05) * gain[...]).astype(BF16)

    for k in (4, 3, 5, 2, 6, 1, 7):
        f_y(k).start()
    loads[4].wait()
    loads[5].wait()
    w_hi[:, :128], w_lo[:, :128] = split(w_self[...])
    w_hi[:, 128:], w_lo[:, 128:] = split(w_neigh[...])
    count(38, 52)
    loop(0, NX, lambda k: r_d(k).wait_recv())
    title = iota((128, 512), 1)
    named = iota((128, 512), 0)
    same = jnp.where((named < 32) & (named // 8 == title % 4), 1.0, 0.0).astype(BF16)
    ahead = jnp.where((named < 32) & (named // 8 < title % 4), 1.0, 0.0).astype(BF16)
    mine = (title // 4) == named
    slot = iota((256, 512), 0)
    col = iota((256, 512), 1)
    match = (
        (slot // 32 == (col % 32) // 4)
        & ((slot % 32) // 4 == (col % 256) // 32)
        & ((slot % 4) // 2 == col // 256)
    )
    wanted = jnp.where(match, (slot % 2).astype(F32) + 1.0, -1.0)

    def select(block):
        listed = rt[block].reshape(128, 128)
        hits = jnp.where(listed == dp.astype(F32), 1.0, 0.0).astype(BF16)
        code = dot(hits, same) * (1.0 + dot(hits, ahead))
        code = jnp.sum(jnp.where(mine, code, 0.0), axis=0, keepdims=True)
        chosen = jnp.where(code == wanted, 1.0, 0.0)
        sel[block] = chosen.astype(BF16)
        sel_t[block] = chosen.T.astype(BF16)

    loop(0, NX, select)

    loop(1, NY, lambda k: f_y(k).wait_recv())
    group_feats = jnp.concatenate([feats[g].astype(F32) for g in range(NY)], axis=0).astype(BF16)
    tg[x, c, z] = (dot(group_feats, w_hi[...]) + dot(group_feats, w_lo[...])).astype(BF16)

    for k in (4, 3, 5):
        t_z(k).start()
    for k in range(1, NX):
        t_s(k, 0).start()
    for k in (2, 6, 1, 7):
        t_z(k).start()
    for k in (1, 7, 2, 6, 3, 5, 4):
        t_z(k).wait_recv()
        for n in range(1, NX):
            t_s(n, NZ - k).start()
    t_d(0).start()
    count(52, 64)
    loop(0, 16, flip)

    def place(block):
        rows = dot(sel[block], tg[block].reshape(512, COLS)).astype(BF16)
        for g in range(NY):
            xs[pl.ds(pl.multiple_of(g * 128 + block * 32, 32), 32), :] = rows[g * 32:(g + 1) * 32]

    t_d(0).wait_recv()
    place(x)
    for k in (1, 3, 2):
        t_x(k).wait_recv()
        t_d(k).start()
    for k in (1, 3, 2):
        t_d(k).wait_recv()
        place((x - k + NX) % NX)

    def layer(step):
        rows = pl.ds(step * 256, 256)
        total = xs[rows, :128].astype(F32) + dot(adj[rows, :], xs[:, 128:]) + bias[...]
        gate = 1.0 / (1.0 + jnp.exp(-total))
        hidden_out[rows, :] = total * gate
        ds[rows, :128] = (cot[rows, :] * gate * (1.0 + total * (1.0 - gate))).astype(BF16)

    for step in range(4):
        layer(step)

    def backward(step):
        rows = pl.ds(step * 256, 256)
        ds[rows, 128:] = dot(adj_t[rows, :], ds[:, :128]).astype(BF16)

    for step in range(4):
        backward(step)

    def titles_of(block):
        rows = jnp.concatenate(
            [ds[pl.ds(pl.multiple_of(g * 128 + block * 32, 32), 32), :] for g in range(NY)], axis=0
        )
        ub[block] = dot(sel_t[block], rows).astype(BF16).reshape(NC, 256, COLS)

    for k in (1, 2, 3, 0):
        titles_of((x + k) % NX)
        u_d(k).start()
    for k in (1, 2, 3):
        to = (x + k) % NX
        u_d(k).wait_recv()
        vs[to] = (ub[to, c].astype(F32) + ur[to].astype(F32)).astype(BF16).reshape(NZ, 32, COLS)
        for dz in (4, 5, 3, 6, 2, 7, 1, 0):
            u_x(k, dz).start()
    u_d(0).wait_recv()
    vs[x] = (ub[x, c].astype(F32) + ur[x].astype(F32)).astype(BF16).reshape(NZ, 32, COLS)

    def gathered(dz):
        total = vs[x, (z + dz) % NZ].astype(F32)
        for k in (1, 3, 2):
            u_x(k, dz).wait_recv()
            total = total + vr[k, dz].astype(F32)
        return total

    for dz in (4, 5, 3, 6, 2, 7, 1):
        yo[dz] = gathered(dz).astype(BF16)
        u_z(dz).start()
    node = gathered(0)
    for k in (1, 7, 2, 6, 3, 5, 4):
        u_z(k).wait_recv()
        node = node + yr[k].astype(F32)
    high, low = split(node)
    partial = dot(high, w_hi[...], NT) + dot(high, w_lo[...], NT) + dot(low, w_hi[...], NT)
    for g in range(NY):
        po[g] = partial[g * 4:(g + 1) * 4].astype(BF16)
    for k in (4, 3, 5, 2, 6, 1, 7):
        p_y(k).start()
    result = po[y].astype(F32)
    for k in range(1, NY):
        p_y(k).wait_recv()
        result = result + pr[k].astype(F32)
    grads_out[...] = result

    loop(1, NX, lambda k: a_x(k).wait_send())
    loop(1, NX, lambda k: b_x(k).wait_send())
    loop(1, NX, lambda k: r_x(k).wait_send())
    loop(1, NX, lambda k: t_x(k).wait_send())
    for k in range(1, NX):
        loop(0, NZ, lambda dz: u_x(k, dz).wait_send())
    loop(1, NZ, lambda k: b_z(k).wait_send())
    loop(1, NZ, lambda k: r_z(k).wait_send())
    loop(1, NZ, lambda k: t_z(k).wait_send())
    loop(1, NZ, lambda k: u_z(k).wait_send())
    loop(1, NY, lambda k: r_y(k).wait_send())
    loop(1, NY, lambda k: f_y(k).wait_send())
    loop(1, NY, lambda k: p_y(k).wait_send())
    loop(0, NX, lambda k: b_d(k).wait_send())
    loop(0, NX, lambda k: r_d(k).wait_send())
    loop(0, NX, lambda k: t_d(k).wait_send())
    loop(0, NX, lambda k: u_d(k).wait_send())
    for step in range(4):
        for way in range(2):
            for sub in range(2):
                if step < 3 or way == sub:
                    a_z(step, way, sub).wait_send()
    a_d(0, 0).wait_send()
    for step in range(1, 5):
        for way in range(2):
            a_d(step, way).wait_send()


def shards(texts, qkv_weight, norm_gain, routes, w_self, w_neigh, gnn_bias, neighbors, cotangent):
    vmem = pl.BlockSpec(memory_space=pltpu.VMEM)
    dma = pltpu.SemaphoreType.DMA
    hidden, grads = pl.pallas_call(
        kernel,
        out_shape=(
            jax.ShapeDtypeStruct((ROWS, 128), F32),
            jax.ShapeDtypeStruct((TITLES, D), F32),
        ),
        in_specs=[pl.BlockSpec(memory_space=pl.ANY)] * 9,
        out_specs=(vmem, vmem),
        scratch_shapes=[
            pltpu.VMEM((TITLES * SEQ, D), BF16),
            pltpu.VMEM((36, D), BF16),
            pltpu.VMEM((1, D), F32),
            pltpu.VMEM((TITLES, 8), jnp.int32),
            pltpu.VMEM((D, 128), F32),
            pltpu.VMEM((D, 128), F32),
            pltpu.VMEM((1, 128), F32),
            pltpu.VMEM((FAN, ROWS), jnp.int32),
            pltpu.VMEM((ROWS, 128), F32),
            dma((9,)),
            pltpu.VMEM((NC, NZ, NX, PIECE_A, 128), BF16),
            pltpu.VMEM((NC, NX, NZ, PIECE_B, 128), BF16),
            pltpu.VMEM((3 * D, D), BF16),
            pltpu.VMEM((3, TITLES, 256, SEQ), BF16),
            pltpu.VMEM((3, TITLES, SEQ, 256), BF16),
            pltpu.VMEM((3, TITLES, SEQ, 256), BF16),
            pltpu.VMEM((12, 8, 256), F32),
            pltpu.VMEM((ROWS, ROWS), BF16),
            pltpu.VMEM((ROWS, ROWS), BF16),
            pltpu.VMEM((D, COLS), BF16),
            pltpu.VMEM((D, COLS), BF16),
            pltpu.VMEM((NY, 8, 128), F32),
            pltpu.VMEM((NX, NC, NZ, 8, 128), F32),
            pltpu.VMEM((NX, 256, 512), BF16),
            pltpu.VMEM((NX, 512, 256), BF16),
            pltpu.VMEM((NY, TITLES, D), BF16),
            pltpu.VMEM((NX, NC, NZ, 32, COLS), BF16),
            pltpu.VMEM((ROWS, COLS), BF16),
            pltpu.VMEM((ROWS, COLS), BF16),
            pltpu.VMEM((NX, NC, 256, COLS), BF16),
            pltpu.VMEM((NX, 256, COLS), BF16),
            pltpu.VMEM((NX, NZ, 32, COLS), BF16),
            pltpu.VMEM((NX, NZ, 32, COLS), BF16),
            pltpu.VMEM((NZ, 32, COLS), BF16),
            pltpu.VMEM((NZ, 32, COLS), BF16),
            pltpu.VMEM((NY, TITLES, D), BF16),
            pltpu.VMEM((NY, TITLES, D), BF16),
            dma((NX,)), dma((NX,)),
            dma((4, 2, 2)), dma((4, 2, 2)),
            dma((5, 2)), dma((5, 2)),
            dma((NZ,)), dma((NZ,)),
            dma((NX,)), dma((NX,)),
            dma((NX,)), dma((NX,)),
            dma((NY,)), dma((NY,)),
            dma((NZ,)), dma((NZ,)),
            dma((NX,)), dma((NX,)),
            dma((NX,)), dma((NX,)),
            dma((NY,)), dma((NY,)),
            dma((NZ,)), dma((NZ,)),
            dma((NX,)), dma((NX,)),
            dma((NX,)), dma((NX,)),
            dma((NX,)), dma((NX,)),
            dma((NX, NZ)), dma((NX, NZ)),
            dma((NZ,)), dma((NZ,)),
            dma((NY,)), dma((NY,)),
        ],
        compiler_params=pltpu.CompilerParams(
            collective_id=0, has_side_effects=True, vmem_limit_bytes=60 * 2**20
        ),
        name="glem_step",
    )(
        texts.reshape(TITLES * SEQ, D),
        qkv_weight.T,
        norm_gain.reshape(1, D),
        routes,
        w_self,
        w_neigh,
        gnn_bias.reshape(1, 128),
        neighbors.T,
        cotangent,
    )
    return hidden, grads


def solution(mesh):
    placed = (
        P(("dp", "graph"), None, None),
        P(None, "dp"),
        P(),
        P(("dp", "graph"), None),
        P(None, "graph"),
        P(None, "graph"),
        P("graph"),
        P("dp", None),
        P("dp", "graph"),
    )
    return jax.shard_map(
        shards,
        mesh=mesh,
        in_specs=placed,
        out_specs=(P("dp", "graph"), P(("dp", "graph"), None)),
        check_vma=False,
    )
```
